128 devices in a mesh: gx: 8 (over y, core), gy: 16 (over z, x).
Axes of the slice: x: 4, y: 4, z: 4, core: 2. Of those that a mesh axis runs over, the one named last changes fastest.
Arguments:
- molar_density_logs: float32 [1024, 53, 2048], P('gx', None, 'gy'), may hold values from -2.5 to -0.5
- scaled_thermal_state: float32 [1024, 2048], P('gx', 'gy'), may hold values from 1.5 to 3
- spreading_rate: float32 [1024, 2048], P('gx', 'gy'), may hold values from 0.2 to 2
- tile_burning_load: int32 [1024, 16], P('gx', 'gy'), may hold values from 0 to 1, as said below
- input_multipliers: int32 [325, 53], replicated, may hold values from 0 to 2, as said below
- output_multipliers: int32 [325, 53], replicated, may hold values from 0 to 2, as said below
- arrhenius_prefactor_logs: float32 [325], replicated, may hold values from 0 to 2
- arrhenius_barrier: float32 [325], replicated, may hold values from 0.5 to 4
- balance_ratio_logs: float32 [325], replicated, may hold values from -1 to 1
- enthalpy_yield: float32 [325], replicated, may hold values from -3 to 3
Outputs:
- new_conc: float32 [1024, 53, 2048], P('gx', None, 'gy')
- new_temp: float32 [1024, 2048], P('gx', 'gy')
The draws below stay inside these ranges and needn't reach their ends.
Inputs may be any that keep to these rules, and one draw needn't show every extreme that they name: `tile_burning_load`: among the 2048 blocks of each group of 128 rows that starts at a multiple of 128, exactly 1024 have cost 1, and in every such group all 128 blocks of some column have cost 1. `input_multipliers`: each row's entries add up to 1 or 2; some entry is 2. `output_multipliers`: each row's entries add up to 1 or 2; some entry is 2.
All inputs are finite; a program needn't handle non-finite values.
Results may differ from the reference program's by a relative error of at most 0.0001.
Values sent between devices are 32-bit elements; how exact they have to be, the bound alone decides.
A program may use at most 192 MiB of HBM per device.

```python
import math
import jax
import jax.numpy as jnp
from jax import lax

S = 53
RATE_LAWS = 325
CX = 128
CY = 128
SUBSTEPS = 4
ACT_DEV = 64
YTILES = 16
GRID_ALPHA_COUNT = 1024
GRID_BETA_COUNT = 2048


def stoich_table(key):
    key_lead, key_second, key_double, key_place = jax.random.split(key, 4)
    leading = jax.random.randint(key_lead, (RATE_LAWS,), 0, S)
    second = jax.random.randint(key_second, (RATE_LAWS,), 0, S)
    doubled = jax.random.randint(key_double, (RATE_LAWS,), 0, 2)
    place = jax.random.randint(key_place, (), 0, RATE_LAWS)
    reaction = jnp.arange(RATE_LAWS)
    doubled = jnp.where(reaction == place, 1, doubled)
    second = jnp.where(reaction == place, leading, second)
    species = jnp.arange(S)
    table = (leading[:, None] == species[None, :]).astype(jnp.int32)
    table = table + doubled[:, None] * (second[:, None] == species[None, :]).astype(jnp.int32)
    return table.astype(jnp.int32)


def draw_input_multipliers(key, part):
    key = jax.random.fold_in(key, 21)
    return stoich_table(key)


def draw_output_multipliers(key, part):
    key = jax.random.fold_in(key, 37)
    return stoich_table(key)


def draw_tile_burning_load(key, part):
    key = jax.random.fold_in(key, 11)
    group_count = GRID_ALPHA_COUNT // CX

    def draw_group(group_key):
        key_front, key_jitter = jax.random.split(group_key)
        front_col = jax.random.randint(key_front, (), 0, YTILES)
        jitter = jax.random.randint(key_jitter, (CX, YTILES), 0, 1024)
        column = jnp.arange(YTILES)
        distance = jnp.minimum((column - front_col) % YTILES, (front_col - column) % YTILES)
        closeness = (YTILES - distance) * 256
        priority = jitter + closeness[None, :]
        priority = jnp.where(column[None, :] == front_col, 16384, priority)
        flat_score = priority.reshape(-1) * (CX * YTILES) + jnp.arange(CX * YTILES)
        unused, chosen = lax.top_k(flat_score.astype(jnp.int32), ACT_DEV * YTILES)
        chosen_mask = jnp.zeros((CX * YTILES,), jnp.int32).at[chosen].set(1)
        return chosen_mask.reshape(CX, YTILES)
    group_keys = jax.random.split(key, group_count)
    return jax.vmap(draw_group)(group_keys).reshape(GRID_ALPHA_COUNT, YTILES).astype(jnp.int32)


def level_of(rng, dims, cuts, low, high):
    gain, own = 1.0, jax.random.fold_in(rng, 6)
    for position, shards_of in cuts:
        draws = jnp.exp(jax.random.uniform(jax.random.fold_in(own, position), (shards_of,), jnp.float32, low / len(cuts), high / len(cuts)))
        gain = gain * jnp.repeat(draws, dims[position] // shards_of).reshape([-1 if axis == position else 1 for axis in range(len(dims))])
    return gain


def scatter_about(own_key, extent, deviation, limit, dtype=jnp.bfloat16):
    return jnp.clip(deviation * jax.random.normal(own_key, extent, jnp.float32), -limit, limit).astype(dtype)


def setup_inputs(seed: int = 0) -> dict:
    splits = jax.random.split(jax.random.key(seed), 11)
    return {
        "molar_density_logs": jnp.clip(-2.5 + 2.0 * jax.random.uniform(splits[0], (GRID_ALPHA_COUNT, S, GRID_BETA_COUNT), jnp.float32) ** level_of(splits[0], (GRID_ALPHA_COUNT, S, GRID_BETA_COUNT), ((0, 8), (2, 16)), -0.2, 0.2), -2.5, -0.5),
        "scaled_thermal_state": jnp.clip(1.5 + 1.5 * jax.random.uniform(splits[1], (GRID_ALPHA_COUNT, GRID_BETA_COUNT), jnp.float32) ** level_of(splits[1], (GRID_ALPHA_COUNT, GRID_BETA_COUNT), ((0, 8), (1, 16)), -0.2, 0.2), 1.5, 3.0),
        "spreading_rate": jnp.clip(jnp.exp(math.log(2.0) - 2.3025851 * jax.random.uniform(splits[2], (GRID_ALPHA_COUNT, GRID_BETA_COUNT), jnp.float32) ** level_of(splits[2], (GRID_ALPHA_COUNT, GRID_BETA_COUNT), ((0, 8), (1, 16)), -0.2, 0.2)), 0.2, 2.0),
        "tile_burning_load": draw_tile_burning_load(jax.random.fold_in(splits[10], 71), 0),
        "input_multipliers": draw_input_multipliers(jax.random.fold_in(splits[10], 71), 0),
        "output_multipliers": draw_output_multipliers(jax.random.fold_in(splits[10], 71), 0),
        "arrhenius_prefactor_logs": jnp.clip(jax.random.uniform(splits[6], (RATE_LAWS,), jnp.float32, 0.0, 2.0), 0.0, 2.0),
        "arrhenius_barrier": jnp.clip(jnp.exp(jax.random.uniform(splits[7], (RATE_LAWS,), jnp.float32, math.log(0.5), math.log(4.0))), 0.5, 4.0),
        "balance_ratio_logs": jnp.clip(jax.random.uniform(splits[8], (RATE_LAWS,), jnp.float32, -1.0, 1.0), -1.0, 1.0),
        "enthalpy_yield": scatter_about(splits[9], (RATE_LAWS,), 0.5, 3.0, jnp.float32),
    }


time_step = 0.01
diffusion_number = 0.1


def kinetics_update(state_bundle, onward_speed, backward_speed, overall_speed, arrhenius_prefactor_logs, arrhenius_barrier, balance_ratio_logs, enthalpy_yield):
    species = state_bundle[:, :-1, :]
    temper = state_bundle[:, -1, :]
    for substep in range(SUBSTEPS):
        reciprocal_value = 1.0 / temper
        onward_speed_logs = arrhenius_prefactor_logs[None, :, None] - arrhenius_barrier[None, :, None] * reciprocal_value[:, None, :]
        forward = jnp.einsum("rs,bsc->brc", onward_speed, species, precision=lax.Precision.HIGHEST)
        backward = jnp.einsum("rs,bsc->brc", backward_speed, species, precision=lax.Precision.HIGHEST)
        net_rate = jnp.exp(onward_speed_logs + forward) - jnp.exp(onward_speed_logs - balance_ratio_logs[None, :, None] + backward)
        change = jnp.einsum("rs,brc->bsc", overall_speed, net_rate, precision=lax.Precision.HIGHEST)
        release = jnp.einsum("r,brc->bc", enthalpy_yield, net_rate, precision=lax.Precision.HIGHEST)
        species = species + time_step * change * jnp.exp(-species)
        temper = temper + time_step * release
    return jnp.concatenate([species, temper[:, None, :]], axis=1)


def transport(padded_state, padded_diff):
    center = padded_state[1:-1, :, 1:-1]
    diff_here = padded_diff[1:-1, :, 1:-1]
    pairs = ((padded_state[:-2, :, 1:-1], padded_diff[:-2, :, 1:-1]),
             (padded_state[2:, :, 1:-1], padded_diff[2:, :, 1:-1]),
             (padded_state[1:-1, :, :-2], padded_diff[1:-1, :, :-2]),
             (padded_state[1:-1, :, 2:], padded_diff[1:-1, :, 2:]))
    flux_sum = jnp.zeros_like(center)
    for neighbor, diff_near in pairs:
        flux_sum = flux_sum + 0.5 * (diff_here + diff_near) * (neighbor - center)
    return center + diffusion_number * flux_sum


def reference(molar_density_logs, scaled_thermal_state, spreading_rate, tile_burning_load, input_multipliers, output_multipliers, arrhenius_prefactor_logs, arrhenius_barrier, balance_ratio_logs, enthalpy_yield):
    state_bundle = jnp.concatenate([molar_density_logs, scaled_thermal_state[:, None, :]], axis=1)
    onward_speed = input_multipliers.astype(jnp.float32)
    backward_speed = output_multipliers.astype(jnp.float32)
    overall_speed = backward_speed - onward_speed

    def react_row(lone_element):
        return kinetics_update(lone_element[None], onward_speed, backward_speed, overall_speed, arrhenius_prefactor_logs, arrhenius_barrier, balance_ratio_logs, enthalpy_yield)[0]

    reacted = lax.map(react_row, state_bundle)
    active = jnp.repeat(tile_burning_load, CY, axis=1) > 0
    blended = jnp.where(active[:, None, :], reacted, state_bundle)
    padded_state = jnp.pad(blended, ((1, 1), (0, 0), (1, 1)), mode="wrap")
    padded_diff = jnp.pad(spreading_rate[:, None, :], ((1, 1), (0, 0), (1, 1)), mode="wrap")
    updated = transport(padded_state, padded_diff)
    return updated[:, :-1, :], updated[:, -1, :]
```

```python
import jax
import jax.numpy as jnp
from jax import lax
from jax.experimental import pallas as pl
from jax.experimental.pallas import tpu as pltpu
from jax.sharding import PartitionSpec as P

SUBSTEPS = 4
TIME_STEP = 0.01
DIFFUSION_NUMBER = 0.1
LOG2E = 1.4426950408889634
LN2 = 0.6931471805599453

CHUNK = 8
SLOTS = 64
FIELD_ROWS = 56
BLOCK = 9
TEMPER_AT = 8

BF16 = jnp.bfloat16
F32 = jnp.float32


def split_pair(x):
    high = x.astype(BF16).astype(F32)
    return high, x - high


def split_three(x):
    first = x.astype(BF16).astype(F32)
    rest = x - first
    second = rest.astype(BF16).astype(F32)
    return first, second, rest - second


def fill_tables(
    forward_ref, backward_ref, law_refs, exponent_table, sum_table, line, stage
):
    species, laws = forward_ref.shape
    total = exponent_table.shape[0]
    padded = total // 2
    wide = stage.shape[1]
    stage[...] = jnp.zeros_like(stage)
    line[...] = jnp.zeros_like(line)
    for index, ref in enumerate(law_refs):
        line[index : index + 1, 0:laws] = ref[...].reshape(1, laws)
    prefactor, barrier, balance, heat = (line[index : index + 1] for index in range(4))
    b1, b2, b3 = split_three((-LOG2E * LOG2E) * barrier)

    def half(table_ref, constant):
        stage[0:species, 0:laws] = table_ref[...].astype(F32)
        stage[SLOTS : SLOTS + species, 0:laws] = table_ref[...].astype(F32)
        for index, piece in enumerate((b1, b2, b3) + split_three(LOG2E * constant)):
            stage[species + index : species + index + 1] = piece
        for index, piece in enumerate((b1, b2)):
            at = SLOTS + species + index
            stage[at : at + 1] = piece
        return stage[...].T[:padded]

    first = half(forward_ref, prefactor)
    second = half(backward_ref, prefactor - balance)
    exponent_table[...] = jnp.concatenate([first, second], axis=0).astype(BF16)

    stage[...] = jnp.zeros_like(stage)
    stage[0:species, 0:laws] = (backward_ref[...] - forward_ref[...]).astype(F32)
    high, low = split_pair(heat)
    stage[species : species + 1] = high
    stage[species + 8 : species + 9] = low
    law = lax.broadcasted_iota(jnp.int32, (wide, total), 0)
    place = lax.broadcasted_iota(jnp.int32, (wide, total), 1)
    chosen = jnp.where(law == (place // 16) * 8 + place % 8, 1.0, 0.0).astype(BF16)
    table = jnp.dot(stage[0:SLOTS].astype(BF16), chosen, preferred_element_type=F32)
    sum_table[...] = table.astype(BF16)


def chemistry_kernel(
    logs_ref,
    temper_ref,
    spread_ref,
    load_ref,
    forward_ref,
    backward_ref,
    prefactor_ref,
    barrier_ref,
    balance_ref,
    heat_ref,
    state_ref,
    row_halo_ref,
    col_halo_ref,
    cells_ref,
    edges,
    exponent_table,
    sum_table,
    line,
    stage,
    in_sem,
    out_sem,
    send_sem,
    recv_sem,
):
    species, rows, width = logs_ref.shape
    chunks = rows // CHUNK
    cells = CHUNK * width
    laws = exponent_table.shape[0] // 2
    gx, gy = lax.axis_index("gx"), lax.axis_index("gy")
    nx, ny = lax.axis_size("gx"), lax.axis_size("gy")
    up = (lax.rem(gx + nx - 1, nx), gy)
    down = (lax.rem(gx + 1, nx), gy)
    left = (gx, lax.rem(gy + ny - 1, ny))
    right = (gx, lax.rem(gy + 1, ny))

    def fetches(chunk):
        at = pl.ds(pl.multiple_of(chunk * CHUNK, CHUNK), CHUNK)
        target = cells_ref.at[chunk]
        return [
            pltpu.make_async_copy(
                logs_ref.at[:, at], target.at[pl.ds(0, species)], in_sem.at[0, chunk]
            ),
            pltpu.make_async_copy(temper_ref.at[at], target.at[species], in_sem.at[1, chunk]),
            pltpu.make_async_copy(spread_ref.at[at], target.at[species + 1], in_sem.at[2, chunk]),
        ]

    def flush(chunk):
        at = pl.ds(pl.multiple_of(chunk * CHUNK, CHUNK), CHUNK)
        return pltpu.make_async_copy(cells_ref.at[chunk], state_ref.at[:, at], out_sem.at[chunk])

    @pl.loop(0, chunks)
    def _(chunk):
        for copy in fetches(chunk):
            copy.start()

    barrier = pltpu.get_barrier_semaphore()
    for neighbour in (up, down, left, right):
        pl.semaphore_signal(
            barrier, inc=1, device_id=neighbour, device_id_type=pl.DeviceIdType.MESH
        )

    steps = jnp.where(load_ref[...] > 0, TIME_STEP * LOG2E, 0.0).astype(F32)
    steps = jnp.broadcast_to(steps, (rows, width)).T
    for chunk in range(chunks):
        cells_ref[chunk, species + 2] = steps[chunk * CHUNK : (chunk + 1) * CHUNK]
    fill_tables(
        forward_ref,
        backward_ref,
        (prefactor_ref, barrier_ref, balance_ref, heat_ref),
        exponent_table,
        sum_table,
        line,
        stage,
    )

    edges[...] = jnp.zeros_like(edges)
    split = FIELD_ROWS - 8
    slot = lax.broadcasted_iota(jnp.int32, (8, cells), 0)
    ones = jnp.where(slot < 3, 1.0, 0.0).astype(F32)
    lane = lax.broadcasted_iota(jnp.int32, (FIELD_ROWS, width), 1)
    flat = cells_ref.reshape(chunks * FIELD_ROWS * CHUNK, width)

    def row_of(chunk, row):
        return pl.ds(chunk * (FIELD_ROWS * CHUNK) + row, FIELD_ROWS, stride=CHUNK)

    @pl.loop(0, chunks)
    def _(chunk):
        for copy in fetches(chunk):
            copy.wait()
        fields = jnp.concatenate([flat[row_of(chunk, row)] for row in range(CHUNK)], axis=1)
        step = fields[FIELD_ROWS - 1 : FIELD_ROWS]
        fields = fields * LOG2E
        for _ in range(SUBSTEPS):
            body, end = fields[:split], fields[split:]
            inverse = jnp.broadcast_to(1.0 / fields[species : species + 1], (8, cells))
            end_operand = jnp.where(slot < species - split, end, inverse)
            high, low = split_pair(jnp.concatenate([body, end_operand], axis=0))
            operand = jnp.concatenate(
                [high, ones, low, jnp.zeros((8, cells), F32)], axis=0
            ).astype(BF16)
            powers = jnp.dot(exponent_table[...], operand, preferred_element_type=F32)
            net = jnp.exp2(powers[:laws]) - jnp.exp2(powers[laws:])
            high, low = split_pair(net)
            pieces = jnp.concatenate(
                [high.reshape(laws // 8, 1, 8, cells), low.reshape(laws // 8, 1, 8, cells)], axis=1
            )
            pieces = pieces.reshape(2 * laws, cells).astype(BF16)
            change = jnp.dot(sum_table[...], pieces, preferred_element_type=F32)
            end_change = change[split:FIELD_ROWS] + change[FIELD_ROWS:]
            end_gain = jnp.where(
                slot < species - split,
                jnp.exp2(-end),
                jnp.where(slot == species - split, 1.0, 0.0),
            )
            body = body + step * (change[:split] * jnp.exp2(-body))
            end = end + step * (end_change * end_gain)
            fields = jnp.concatenate([body, end], axis=0)

        fields = fields * LN2
        base = chunk * CHUNK
        first = jnp.zeros((FIELD_ROWS, width), F32)
        last = jnp.zeros((FIELD_ROWS, width), F32)
        for row in range(CHUNK):
            body = fields[:, row * width : (row + 1) * width]
            flat[row_of(chunk, row)] = body
            first = jnp.where(lane == row, pltpu.roll(body, row, 1), first)
            last = jnp.where(lane == row, pltpu.roll(body, row + 1, 1), last)
        mine = (lane >= base) & (lane < base + CHUNK)
        edges[0] = jnp.where(mine, pltpu.roll(first, base, 1), edges[0])
        edges[1] = jnp.where(mine, pltpu.roll(last, base, 1), edges[1])
        flush(chunk).start()

    edges[2] = flat[row_of(0, 0)]
    edges[3] = flat[row_of(chunks - 1, CHUNK - 1)]
    pl.semaphore_wait(barrier, 4)
    sends = []
    for index, (source, target, device) in enumerate(
        (
            (edges.at[3], row_halo_ref.at[0], down),
            (edges.at[2], row_halo_ref.at[1], up),
            (edges.at[1], col_halo_ref.at[0], right),
            (edges.at[0], col_halo_ref.at[1], left),
        )
    ):
        sends.append(
            pltpu.make_async_remote_copy(
                src_ref=source,
                dst_ref=target,
                send_sem=send_sem.at[index],
                recv_sem=recv_sem.at[index],
                device_id=device,
                device_id_type=pl.DeviceIdType.MESH,
            )
        )
    for copy in sends:
        copy.start()

    @pl.loop(0, chunks)
    def _(chunk):
        flush(chunk).wait()

    for copy in sends:
        copy.wait()


def transport_kernel(
    state_ref, spread_ref, row_halo_ref, col_halo_ref, conc_ref, temp_ref, gains, sides, sheet
):
    block, rows, width = state_ref.shape
    turn = pl.program_id(0)
    row = lax.broadcasted_iota(jnp.int32, (rows, width), 0)
    lane = lax.broadcasted_iota(jnp.int32, (rows, width), 1)
    spread_slot = FIELD_ROWS - 2

    def around(here, component):
        north = jnp.where(row == 0, row_halo_ref[0, component], pltpu.roll(here, 1, 0))
        south = jnp.where(
            row == rows - 1, row_halo_ref[1, component], pltpu.roll(here, rows - 1, 0)
        )
        side = pltpu.roll(sides[...], width - 1 - 2 * component, 1)
        west = pltpu.roll(jnp.where(lane == width - 1, side, here), 1, 1)
        east = pltpu.roll(jnp.where(lane == 0, side, here), width - 1, 1)
        return north, south, west, east

    @pl.when(turn == 0)
    def _():
        sheet[...] = jnp.zeros_like(sheet)
        sheet[pl.ds(0, FIELD_ROWS, stride=2)] = col_halo_ref[0]
        sheet[pl.ds(1, FIELD_ROWS, stride=2)] = col_halo_ref[1]
        sides[...] = sheet[...].T
        here = spread_ref[...]
        rest = jnp.ones_like(here)
        for index, near in enumerate(around(here, spread_slot)):
            gain = (0.5 * DIFFUSION_NUMBER) * (here + near)
            gains[index] = gain
            rest = rest - gain
        gains[4] = rest

    for index in range(block):
        here = state_ref[index]
        new = gains[4] * here
        for which, near in enumerate(around(here, turn * block + index)):
            new = new + gains[which] * near
        conc_ref[index] = new

        if index == TEMPER_AT:

            @pl.when(turn == pl.num_programs(0) - 1)
            def _():
                temp_ref[...] = new


def per_device(
    molar_density_logs,
    scaled_thermal_state,
    spreading_rate,
    tile_burning_load,
    input_multipliers,
    output_multipliers,
    arrhenius_prefactor_logs,
    arrhenius_barrier,
    balance_ratio_logs,
    enthalpy_yield,
):
    rows, species, width = molar_density_logs.shape
    laws = input_multipliers.shape[0]
    padded = -(-laws // 8) * 8
    wide = -(-laws // 128) * 128
    chunks = rows // CHUNK
    vmem = pl.BlockSpec(memory_space=pltpu.VMEM)
    anywhere = pl.BlockSpec(memory_space=pl.ANY)
    halo = jax.ShapeDtypeStruct((2, FIELD_ROWS, width), F32)
    state, row_halo, col_halo = pl.pallas_call(
        chemistry_kernel,
        out_shape=(jax.ShapeDtypeStruct((FIELD_ROWS, rows, width), F32), halo, halo),
        in_specs=[anywhere] * 3 + [vmem] * 7,
        out_specs=(anywhere,) * 3,
        scratch_shapes=[
            pltpu.VMEM((chunks, FIELD_ROWS, CHUNK, width), F32),
            pltpu.VMEM((4, FIELD_ROWS, width), F32),
            pltpu.VMEM((2 * padded, 2 * SLOTS), BF16),
            pltpu.VMEM((SLOTS, 2 * padded), BF16),
            pltpu.VMEM((8, wide), F32),
            pltpu.VMEM((2 * SLOTS, wide), F32),
            pltpu.SemaphoreType.DMA((3, chunks)),
            pltpu.SemaphoreType.DMA((chunks,)),
            pltpu.SemaphoreType.DMA((4,)),
            pltpu.SemaphoreType.DMA((4,)),
        ],
        compiler_params=pltpu.CompilerParams(
            collective_id=0, has_side_effects=True, vmem_limit_bytes=60 * 2**20
        ),
        name="chemistry",
    )(
        jnp.transpose(molar_density_logs, (1, 0, 2)),
        scaled_thermal_state,
        spreading_rate,
        tile_burning_load.reshape(1, rows),
        input_multipliers.T,
        output_multipliers.T,
        arrhenius_prefactor_logs,
        arrhenius_barrier,
        balance_ratio_logs,
        enthalpy_yield,
    )

    turns = (species + 1) // BLOCK
    plane = pl.BlockSpec((rows, width), lambda i: (0, 0))
    halo = pl.BlockSpec((2, FIELD_ROWS, width), lambda i: (0, 0, 0))
    block = pl.BlockSpec((BLOCK, rows, width), lambda i: (i, 0, 0))
    conc, temp = pl.pallas_call(
        transport_kernel,
        grid=(turns,),
        out_shape=(
            jax.ShapeDtypeStruct((species, rows, width), F32),
            jax.ShapeDtypeStruct((rows, width), F32),
        ),
        in_specs=[block, plane, halo, halo],
        out_specs=(block, plane),
        scratch_shapes=[
            pltpu.VMEM((5, rows, width), F32),
            pltpu.VMEM((rows, width), F32),
            pltpu.VMEM((width, rows), F32),
        ],
        compiler_params=pltpu.CompilerParams(vmem_limit_bytes=60 * 2**20),
        name="transport",
    )(state, spreading_rate, row_halo, col_halo)
    return jnp.transpose(conc, (1, 0, 2)), temp


def solution(mesh):
    placed = (
        P("gx", None, "gy"),
        P("gx", "gy"),
        P("gx", "gy"),
        P("gx", "gy"),
        P(),
        P(),
        P(),
        P(),
        P(),
        P(),
    )
    return jax.shard_map(
        per_device,
        mesh=mesh,
        in_specs=placed,
        out_specs=(P("gx", None, "gy"), P("gx", "gy")),
        check_vma=False,
    )
```

```python
import jax
import jax.numpy as jnp
from jax import lax
from jax.experimental import pallas as pl
from jax.experimental.pallas import tpu as pltpu
from jax.sharding import PartitionSpec as P

SUBSTEPS = 4
TIME_STEP = 0.01
DIFFUSION_NUMBER = 0.1
LOG2E = 1.4426950408889634
LN2 = 0.6931471805599453

CHUNK = 8
SLOTS = 64
FIELD_ROWS = 56
BLOCK = 6
UP, DOWN, LEFT, RIGHT = range(4)

BF16 = jnp.bfloat16
F32 = jnp.float32


def split_pair(x):
    high = x.astype(BF16).astype(F32)
    return high, x - high


def split_three(x):
    first = x.astype(BF16).astype(F32)
    rest = x - first
    second = rest.astype(BF16).astype(F32)
    return first, second, rest - second


def fill_tables(
    forward_ref, backward_ref, law_refs, exponent_table, sum_table, line, stage
):
    species, laws = forward_ref.shape
    total = exponent_table.shape[0]
    padded = total // 2
    wide = stage.shape[1]
    stage[...] = jnp.zeros_like(stage)
    line[...] = jnp.zeros_like(line)
    for index, ref in enumerate(law_refs):
        line[index : index + 1, 0:laws] = ref[...].reshape(1, laws)
    prefactor, barrier, balance, heat = (line[index : index + 1] for index in range(4))
    b1, b2, b3 = split_three((-LOG2E * LOG2E) * barrier)

    def table(table_ref, constant):
        stage[0:species, 0:laws] = table_ref[...].astype(F32)
        stage[SLOTS : SLOTS + species, 0:laws] = table_ref[...].astype(F32)
        for index, piece in enumerate((b1, b2, b3) + split_three(LOG2E * constant)):
            stage[species + index : species + index + 1] = piece
        for index, piece in enumerate((b1, b2)):
            at = SLOTS + species + index
            stage[at : at + 1] = piece
        return stage[...].T[:padded]

    first = table(forward_ref, prefactor)
    second = table(backward_ref, prefactor - balance)
    pairs = [half.reshape(padded // 8, 1, 8, 2 * SLOTS) for half in (first, second)]
    pairs = jnp.concatenate(pairs, axis=1).reshape(total, 2 * SLOTS)
    exponent_table[...] = pairs.astype(BF16)

    stage[...] = jnp.zeros_like(stage)
    stage[0:species, 0:laws] = (backward_ref[...] - forward_ref[...]).astype(F32)
    high, low = split_pair(heat)
    stage[species : species + 1] = high
    stage[species + 8 : species + 9] = low
    law = lax.broadcasted_iota(jnp.int32, (wide, total), 0)
    place = lax.broadcasted_iota(jnp.int32, (wide, total), 1)
    chosen = jnp.where(law == (place // 16) * 8 + place % 8, 1.0, 0.0).astype(BF16)
    spread = jnp.dot(stage[0:SLOTS].astype(BF16), chosen, preferred_element_type=F32)
    sum_table[...] = spread.astype(BF16)


def chemistry_kernel(
    logs_ref,
    temper_ref,
    spread_ref,
    load_ref,
    forward_ref,
    backward_ref,
    prefactor_ref,
    barrier_ref,
    balance_ref,
    heat_ref,
    state_ref,
    halo_ref,
    cells_ref,
    edges,
    halos,
    exponent_table,
    sum_table,
    line,
    stage,
    fields_a,
    fields_b,
    operand_a,
    operand_b,
    net_a,
    net_b,
    in_sem,
    out_sem,
    halo_sem,
    send_sem,
    recv_sem,
):
    species, rows, width = logs_ref.shape
    chunks = rows // CHUNK
    cells = CHUNK * width
    laws = exponent_table.shape[0] // 2
    gx, gy = lax.axis_index("gx"), lax.axis_index("gy")
    nx, ny = lax.axis_size("gx"), lax.axis_size("gy")
    up = (lax.rem(gx + nx - 1, nx), gy)
    down = (lax.rem(gx + 1, nx), gy)
    left = (gx, lax.rem(gy + ny - 1, ny))
    right = (gx, lax.rem(gy + 1, ny))

    def fetches(chunk):
        at = pl.ds(pl.multiple_of(chunk * CHUNK, CHUNK), CHUNK)
        target = cells_ref.at[chunk]
        return [
            pltpu.make_async_copy(
                logs_ref.at[:, at], target.at[pl.ds(0, species)], in_sem.at[0, chunk]
            ),
            pltpu.make_async_copy(temper_ref.at[at], target.at[species], in_sem.at[1, chunk]),
            pltpu.make_async_copy(spread_ref.at[at], target.at[species + 1], in_sem.at[2, chunk]),
        ]

    def flush(chunk):
        at = pl.ds(pl.multiple_of(chunk * CHUNK, CHUNK), CHUNK)
        return pltpu.make_async_copy(cells_ref.at[chunk], state_ref.at[:, at], out_sem.at[chunk])

    def sends():
        copies = []
        for place, device in ((UP, down), (DOWN, up), (LEFT, right), (RIGHT, left)):
            copies.append(
                pltpu.make_async_remote_copy(
                    src_ref=edges.at[place],
                    dst_ref=halos.at[place],
                    send_sem=send_sem.at[place],
                    recv_sem=recv_sem.at[place],
                    device_id=device,
                    device_id_type=pl.DeviceIdType.MESH,
                )
            )
        return copies

    @pl.loop(0, chunks)
    def _(chunk):
        for copy in fetches(chunk):
            copy.start()

    barrier = pltpu.get_barrier_semaphore()
    for neighbour in (up, down, left, right):
        pl.semaphore_signal(
            barrier, inc=1, device_id=neighbour, device_id_type=pl.DeviceIdType.MESH
        )

    steps = jnp.where(load_ref[...] > 0, TIME_STEP * LOG2E, 0.0).astype(F32)
    steps = jnp.broadcast_to(steps, (rows, width)).T
    for chunk in range(chunks):
        cells_ref[chunk, species + 2] = steps[chunk * CHUNK : (chunk + 1) * CHUNK]
    fill_tables(
        forward_ref,
        backward_ref,
        (prefactor_ref, barrier_ref, balance_ref, heat_ref),
        exponent_table,
        sum_table,
        line,
        stage,
    )

    edges[...] = jnp.zeros_like(edges)
    split = FIELD_ROWS - 8
    lane = lax.broadcasted_iota(jnp.int32, (FIELD_ROWS, width), 1)
    flat = cells_ref.reshape((chunks + 1) * FIELD_ROWS * CHUNK, width)

    def row_of(chunk, row):
        return pl.ds(chunk * (FIELD_ROWS * CHUNK) + row, FIELD_ROWS, stride=CHUNK)

    def slots(like):
        return lax.broadcasted_iota(jnp.int32, (8, like.shape[1]), 0)

    def operand_of(body, end):
        slot = slots(end)
        inverse = 1.0 / end[species - split : species - split + 1]
        inverse = jnp.broadcast_to(inverse, end.shape)
        end = jnp.where(slot < species - split, end, inverse)
        high, low = split_pair(jnp.concatenate([body, end], axis=0))
        ones = jnp.where(slot < 3, 1.0, 0.0).astype(F32)
        parts = [high, ones, low, jnp.zeros_like(ones)]
        return jnp.concatenate(parts, axis=0).astype(BF16)

    def load(fields, fields_ref, operand_ref):
        body, end = fields[:split] * LOG2E, fields[split:]
        end = jnp.where(slots(end) == 7, end, end * LOG2E)
        fields_ref[0:split] = body
        fields_ref[split:FIELD_ROWS] = end
        operand_ref[...] = operand_of(body, end)

    def chunk_of(chunk):
        return jnp.concatenate([flat[row_of(chunk, row)] for row in range(CHUNK)], axis=1)

    def rates(operand_ref, net_ref):
        powers = jnp.dot(exponent_table[...], operand_ref[...], preferred_element_type=F32)
        count = powers.shape[1]
        powers = powers.reshape(laws // 8, 2, 8, count)
        net = jnp.exp2(powers[:, 0]) - jnp.exp2(powers[:, 1])
        high, low = split_pair(net)
        pieces = jnp.concatenate([high[:, None], low[:, None]], axis=1)
        net_ref[...] = pieces.reshape(2 * laws, count).astype(BF16)

    def advance(net_ref, fields_ref):
        change = jnp.dot(sum_table[...], net_ref[...], preferred_element_type=F32)
        end_change = change[split:FIELD_ROWS] + change[FIELD_ROWS:]
        body, end = fields_ref[0:split], fields_ref[split:FIELD_ROWS]
        slot = slots(end)
        step = end[7:8]
        gain = jnp.where(
            slot < species - split,
            jnp.exp2(-end),
            jnp.where(slot == species - split, 1.0, 0.0),
        )
        body = body + step * (change[:split] * jnp.exp2(-body))
        end = end + step * (end_change * gain)
        return body, end

    def renew(net_ref, fields_ref, operand_ref):
        body, end = advance(net_ref, fields_ref)
        fields_ref[0:split] = body
        fields_ref[split:FIELD_ROWS] = end
        operand_ref[...] = operand_of(body, end)

    def finish(chunk, body, end):
        fields = jnp.concatenate([body, end], axis=0) * LN2
        for row in range(CHUNK):
            flat[row_of(chunk, row)] = fields[:, row * width : (row + 1) * width]

    def collect(chunk):
        base = chunk * CHUNK
        first = jnp.zeros((FIELD_ROWS, width), F32)
        last = jnp.zeros((FIELD_ROWS, width), F32)
        for row in range(CHUNK):
            part = flat[row_of(chunk, row)]
            first = jnp.where(lane == row, pltpu.roll(part, row, 1), first)
            last = jnp.where(lane == row, pltpu.roll(part, row + 1, 1), last)
        mine = (lane >= base) & (lane < base + CHUNK)
        edges[RIGHT] = jnp.where(mine, pltpu.roll(first, base, 1), edges[RIGHT])
        edges[LEFT] = jnp.where(mine, pltpu.roll(last, base, 1), edges[LEFT])

    def arrive(chunk):
        for copy in fetches(chunk):
            copy.wait()

    arrive(0)
    collect(0)
    edges[DOWN] = flat[row_of(0, 0)]
    load(chunk_of(0), fields_a, operand_a)
    fields_b[...] = jnp.ones_like(fields_b)
    net_b[...] = jnp.zeros_like(net_b)
    pairs = chunks // 2

    @pl.loop(0, pairs)
    def _(pair):
        a, b = 2 * pair, 2 * pair + 1

        @pl.when(pair == 0)
        def _():
            arrive(1)
            arrive(2)

        @pl.when(pair == 1)
        def _():
            collect(1)
            collect(2)

            @pl.loop(3, chunks)
            def _(chunk):
                arrive(chunk)
                collect(chunk)

            edges[UP] = flat[row_of(chunks - 1, CHUNK - 1)]
            pl.semaphore_wait(barrier, 4)
            for copy in sends():
                copy.start()

        @pl.when(pair > 0)
        def _():
            flush(a - 2).start()

        @pl.when(pair > 1)
        def _():
            flush(b - 4).start()

        for substep in range(SUBSTEPS):
            rates(operand_a, net_a)
            if substep == 0:
                finish(jnp.where(pair == 0, chunks, b - 2), *advance(net_b, fields_b))
                load(chunk_of(b), fields_b, operand_b)
            else:
                renew(net_b, fields_b, operand_b)
            rates(operand_b, net_b)
            if substep == SUBSTEPS - 1:
                finish(a, *advance(net_a, fields_a))
                load(chunk_of(jnp.minimum(a + 2, chunks - 1)), fields_a, operand_a)
            else:
                renew(net_a, fields_a, operand_a)

    flush(chunks - 3).start()
    flush(chunks - 2).start()
    finish(chunks - 1, *advance(net_b, fields_b))
    flush(chunks - 1).start()

    for copy in sends():
        copy.wait()
    count = 4 * width
    fields_h, operand_h, net_h = (
        ref.at[:, pl.ds(0, count)] for ref in (fields_a, operand_a, net_a)
    )
    load(jnp.concatenate([halos[place] for place in range(4)], axis=1), fields_h, operand_h)
    for _ in range(SUBSTEPS):
        rates(operand_h, net_h)
        renew(net_h, fields_h, operand_h)
    for place in range(4):
        edges[place] = fields_h[:, place * width : (place + 1) * width] * LN2
    copy = pltpu.make_async_copy(edges, halo_ref, halo_sem)
    copy.start()

    @pl.loop(0, chunks)
    def _(chunk):
        flush(chunk).wait()

    copy.wait()


def transport_kernel(
    state_ref,
    spread_ref,
    halo_ref,
    conc_ref,
    temp_ref,
    old,
    new,
    gains,
    sides,
    sheet,
    in_sem,
    out_sem,
    temp_sem,
):
    species, rows, width = conc_ref.shape
    blocks = (species + 1) // BLOCK
    row = lax.broadcasted_iota(jnp.int32, (rows, width), 0)
    lane = lax.broadcasted_iota(jnp.int32, (rows, width), 1)

    def fetch(block):
        at = pl.ds(block * BLOCK, BLOCK)
        return pltpu.make_async_copy(state_ref.at[at], old.at[at], in_sem.at[block])

    def flush(block, count):
        at = pl.ds(block * BLOCK, count)
        return pltpu.make_async_copy(new.at[at], conc_ref.at[at], out_sem.at[block])

    def flush_temper():
        return pltpu.make_async_copy(new.at[species], temp_ref, temp_sem)

    @pl.loop(0, blocks)
    def _(block):
        fetch(block).start()

    def around(here, component):
        north = jnp.where(row == 0, halo_ref[UP, component], pltpu.roll(here, 1, 0))
        south = jnp.where(
            row == rows - 1, halo_ref[DOWN, component], pltpu.roll(here, rows - 1, 0)
        )
        side = pltpu.roll(sides[...], width - 1 - 2 * component, 1)
        west = jnp.where(lane == 0, side, pltpu.roll(here, 1, 1))
        east = jnp.where(lane == width - 1, side, pltpu.roll(here, width - 1, 1))
        return north, south, west, east

    sheet[...] = jnp.zeros_like(sheet)
    sheet[pl.ds(0, FIELD_ROWS, stride=2)] = halo_ref[RIGHT]
    sheet[pl.ds(1, FIELD_ROWS, stride=2)] = halo_ref[LEFT]
    sides[...] = sheet[...].T
    here = spread_ref[...]
    rest = jnp.ones_like(here)
    for index, near in enumerate(around(here, FIELD_ROWS - 2)):
        gain = (0.5 * DIFFUSION_NUMBER) * (here + near)
        gains[index] = gain
        rest = rest - gain
    gains[4] = rest

    @pl.loop(0, blocks)
    def _(block):
        fetch(block).wait()
        for index in range(BLOCK):
            component = block * BLOCK + index
            here = old[component]
            total = gains[4] * here
            for which, near in enumerate(around(here, component)):
                total = total + gains[which] * near
            new[component] = total

        @pl.when(block < blocks - 1)
        def _():
            flush(block, BLOCK).start()

    flush(blocks - 1, BLOCK - 1).start()
    flush_temper().start()

    @pl.loop(0, blocks - 1)
    def _(block):
        flush(block, BLOCK).wait()

    flush(blocks - 1, BLOCK - 1).wait()
    flush_temper().wait()


def per_device(
    molar_density_logs,
    scaled_thermal_state,
    spreading_rate,
    tile_burning_load,
    input_multipliers,
    output_multipliers,
    arrhenius_prefactor_logs,
    arrhenius_barrier,
    balance_ratio_logs,
    enthalpy_yield,
):
    rows, species, width = molar_density_logs.shape
    laws = input_multipliers.shape[0]
    padded = -(-laws // 8) * 8
    wide = -(-laws // 128) * 128
    chunks = rows // CHUNK
    cells = CHUNK * width
    vmem = pl.BlockSpec(memory_space=pltpu.VMEM)
    anywhere = pl.BlockSpec(memory_space=pl.ANY)
    state, halo = pl.pallas_call(
        chemistry_kernel,
        out_shape=(
            jax.ShapeDtypeStruct((FIELD_ROWS, rows, width), F32),
            jax.ShapeDtypeStruct((4, FIELD_ROWS, width), F32),
        ),
        in_specs=[anywhere] * 3 + [vmem] * 7,
        out_specs=(anywhere,) * 2,
        scratch_shapes=[
            pltpu.VMEM((chunks + 1, FIELD_ROWS, CHUNK, width), F32),
            pltpu.VMEM((4, FIELD_ROWS, width), F32),
            pltpu.VMEM((4, FIELD_ROWS, width), F32),
            pltpu.VMEM((2 * padded, 2 * SLOTS), BF16),
            pltpu.VMEM((SLOTS, 2 * padded), BF16),
            pltpu.VMEM((8, wide), F32),
            pltpu.VMEM((2 * SLOTS, wide), F32),
            pltpu.VMEM((FIELD_ROWS, cells), F32),
            pltpu.VMEM((FIELD_ROWS, cells), F32),
            pltpu.VMEM((2 * SLOTS, cells), BF16),
            pltpu.VMEM((2 * SLOTS, cells), BF16),
            pltpu.VMEM((2 * padded, cells), BF16),
            pltpu.VMEM((2 * padded, cells), BF16),
            pltpu.SemaphoreType.DMA((3, chunks)),
            pltpu.SemaphoreType.DMA((chunks,)),
            pltpu.SemaphoreType.DMA(()),
            pltpu.SemaphoreType.DMA((4,)),
            pltpu.SemaphoreType.DMA((4,)),
        ],
        compiler_params=pltpu.CompilerParams(
            collective_id=0, has_side_effects=True, vmem_limit_bytes=60 * 2**20
        ),
        name="chemistry",
    )(
        jnp.transpose(molar_density_logs, (1, 0, 2)),
        scaled_thermal_state,
        spreading_rate,
        tile_burning_load.reshape(1, rows),
        input_multipliers.T,
        output_multipliers.T,
        arrhenius_prefactor_logs,
        arrhenius_barrier,
        balance_ratio_logs,
        enthalpy_yield,
    )

    blocks = (species + 1) // BLOCK
    conc, temp = pl.pallas_call(
        transport_kernel,
        out_shape=(
            jax.ShapeDtypeStruct((species, rows, width), F32),
            jax.ShapeDtypeStruct((rows, width), F32),
        ),
        in_specs=[anywhere, vmem, vmem],
        out_specs=(anywhere, anywhere),
        scratch_shapes=[
            pltpu.VMEM((species + 1, rows, width), F32),
            pltpu.VMEM((species + 1, rows, width), F32),
            pltpu.VMEM((5, rows, width), F32),
            pltpu.VMEM((rows, width), F32),
            pltpu.VMEM((width, rows), F32),
            pltpu.SemaphoreType.DMA((blocks,)),
            pltpu.SemaphoreType.DMA((blocks,)),
            pltpu.SemaphoreType.DMA(()),
        ],
        compiler_params=pltpu.CompilerParams(vmem_limit_bytes=60 * 2**20),
        name="transport",
    )(state, spreading_rate, halo)
    return jnp.transpose(conc, (1, 0, 2)), temp


def solution(mesh):
    placed = (
        P("gx", None, "gy"),
        P("gx", "gy"),
        P("gx", "gy"),
        P("gx", "gy"),
        P(),
        P(),
        P(),
        P(),
        P(),
        P(),
    )
    return jax.shard_map(
        per_device,
        mesh=mesh,
        in_specs=placed,
        out_specs=(P("gx", None, "gy"), P("gx", "gy")),
        check_vma=False,
    )
```

```python
import jax
import jax.numpy as jnp
from jax import lax
from jax.experimental import pallas as pl
from jax.experimental.pallas import tpu as pltpu
from jax.sharding import PartitionSpec as P

SUBSTEPS = 4
TIME_STEP = 0.01
DIFFUSION_NUMBER = 0.1
LOG2E = 1.4426950408889634
LN2 = 0.6931471805599453

CHUNK = 8
AHEAD = 4
SLOTS = 64
FIELD_ROWS = 56
BLOCK = 6
UP, DOWN, LEFT, RIGHT = range(4)

BF16 = jnp.bfloat16
F32 = jnp.float32


def split_pair(x):
    high = x.astype(BF16).astype(F32)
    return high, x - high


def split_three(x):
    first = x.astype(BF16).astype(F32)
    rest = x - first
    second = rest.astype(BF16).astype(F32)
    return first, second, rest - second


def fill_tables(
    forward_ref, backward_ref, law_refs, exponent_table, sum_table, line, stage
):
    species, laws = forward_ref.shape
    total = exponent_table.shape[0]
    padded = total // 2
    wide = stage.shape[1]
    stage[...] = jnp.zeros_like(stage)
    line[...] = jnp.zeros_like(line)
    for index, ref in enumerate(law_refs):
        line[index : index + 1, 0:laws] = ref[...].reshape(1, laws)
    prefactor, barrier, balance, heat = (line[index : index + 1] for index in range(4))
    b1, b2, b3 = split_three((-LOG2E * LOG2E) * barrier)

    def table(table_ref, constant):
        stage[0:species, 0:laws] = table_ref[...].astype(F32)
        stage[SLOTS : SLOTS + species, 0:laws] = table_ref[...].astype(F32)
        for index, piece in enumerate((b1, b2, b3) + split_three(LOG2E * constant)):
            stage[species + index : species + index + 1] = piece
        for index, piece in enumerate((b1, b2)):
            at = SLOTS + species + index
            stage[at : at + 1] = piece
        return stage[...].T[:padded]

    first = table(forward_ref, prefactor)
    second = table(backward_ref, prefactor - balance)
    pairs = [half.reshape(padded // 8, 1, 8, 2 * SLOTS) for half in (first, second)]
    pairs = jnp.concatenate(pairs, axis=1).reshape(total, 2 * SLOTS)
    exponent_table[...] = pairs.astype(BF16)

    stage[...] = jnp.zeros_like(stage)
    stage[0:species, 0:laws] = (backward_ref[...] - forward_ref[...]).astype(F32)
    high, low = split_pair(heat)
    stage[species : species + 1] = high
    stage[species + 8 : species + 9] = low
    law = lax.broadcasted_iota(jnp.int32, (wide, total), 0)
    place = lax.broadcasted_iota(jnp.int32, (wide, total), 1)
    chosen = jnp.where(law == (place // 16) * 8 + place % 8, 1.0, 0.0).astype(BF16)
    spread = jnp.dot(stage[0:SLOTS].astype(BF16), chosen, preferred_element_type=F32)
    sum_table[...] = spread.astype(BF16)


def chemistry_kernel(
    logs_ref,
    temper_ref,
    spread_ref,
    load_input,
    forward_input,
    backward_input,
    prefactor_input,
    barrier_input,
    balance_input,
    heat_input,
    state_ref,
    halo_ref,
    cells_ref,
    load_ref,
    forward_ref,
    backward_ref,
    prefactor_ref,
    barrier_ref,
    balance_ref,
    heat_ref,
    edges,
    halos,
    sides,
    exponent_table,
    sum_table,
    line,
    stage,
    fields_a,
    fields_b,
    operand_a,
    operand_b,
    net_a,
    net_b,
    small_sem,
    in_sem,
    out_sem,
    halo_sem,
    send_sem,
    recv_sem,
):
    species, rows, width = logs_ref.shape
    chunks = rows // CHUNK
    cells = CHUNK * width
    laws = exponent_table.shape[0] // 2
    gx, gy = lax.axis_index("gx"), lax.axis_index("gy")
    nx, ny = lax.axis_size("gx"), lax.axis_size("gy")
    up = (lax.rem(gx + nx - 1, nx), gy)
    down = (lax.rem(gx + 1, nx), gy)
    left = (gx, lax.rem(gy + ny - 1, ny))
    right = (gx, lax.rem(gy + 1, ny))

    def fetches(chunk):
        at = pl.ds(pl.multiple_of(chunk * CHUNK, CHUNK), CHUNK)
        target = cells_ref.at[chunk]
        return [
            pltpu.make_async_copy(
                logs_ref.at[:, at], target.at[pl.ds(0, species)], in_sem.at[0, chunk]
            ),
            pltpu.make_async_copy(temper_ref.at[at], target.at[species], in_sem.at[1, chunk]),
            pltpu.make_async_copy(spread_ref.at[at], target.at[species + 1], in_sem.at[2, chunk]),
        ]

    def flush(chunk):
        at = pl.ds(pl.multiple_of(chunk * CHUNK, CHUNK), CHUNK)
        return pltpu.make_async_copy(cells_ref.at[chunk], state_ref.at[:, at], out_sem.at[chunk])

    def sends():
        copies = []
        for place, device in ((UP, down), (DOWN, up), (LEFT, right), (RIGHT, left)):
            copies.append(
                pltpu.make_async_remote_copy(
                    src_ref=edges.at[place],
                    dst_ref=halos.at[place],
                    send_sem=send_sem.at[place],
                    recv_sem=recv_sem.at[place],
                    device_id=device,
                    device_id_type=pl.DeviceIdType.MESH,
                )
            )
        return copies

    pairs_of = (
        (load_input, load_ref),
        (forward_input, forward_ref),
        (backward_input, backward_ref),
        (prefactor_input, prefactor_ref),
        (barrier_input, barrier_ref),
        (balance_input, balance_ref),
        (heat_input, heat_ref),
    )
    smalls = [
        pltpu.make_async_copy(source, target, small_sem.at[index])
        for index, (source, target) in enumerate(pairs_of)
    ]
    for copy in smalls + fetches(0):
        copy.start()

    @pl.loop(1, chunks)
    def _(chunk):
        for copy in fetches(chunk):
            copy.start()

    barrier = pltpu.get_barrier_semaphore()
    for neighbour in (up, down, left, right):
        pl.semaphore_signal(
            barrier, inc=1, device_id=neighbour, device_id_type=pl.DeviceIdType.MESH
        )

    for copy in smalls:
        copy.wait()
    steps = jnp.where(load_ref[...] > 0, TIME_STEP * LOG2E, 0.0).astype(F32)
    steps = jnp.broadcast_to(steps, (rows, width)).T
    for chunk in range(chunks):
        cells_ref[chunk, species + 2] = steps[chunk * CHUNK : (chunk + 1) * CHUNK]
    fill_tables(
        forward_ref,
        backward_ref,
        (prefactor_ref, barrier_ref, balance_ref, heat_ref),
        exponent_table,
        sum_table,
        line,
        stage,
    )

    sides[...] = jnp.zeros_like(sides)
    cells_ref[chunks] = jnp.zeros(cells_ref.shape[1:], F32)
    split = FIELD_ROWS - 8
    lane = lax.broadcasted_iota(jnp.int32, (FIELD_ROWS, width), 1)
    flat = cells_ref.reshape((chunks + 1) * FIELD_ROWS * CHUNK, width)

    def row_of(chunk, row):
        return pl.ds(chunk * (FIELD_ROWS * CHUNK) + row, FIELD_ROWS, stride=CHUNK)

    def slots(like):
        return lax.broadcasted_iota(jnp.int32, (8, like.shape[1]), 0)

    def operand_of(body, end):
        slot = slots(end)
        inverse = 1.0 / end[species - split : species - split + 1]
        inverse = jnp.broadcast_to(inverse, end.shape)
        end = jnp.where(slot < species - split, end, inverse)
        high, low = split_pair(jnp.concatenate([body, end], axis=0))
        ones = jnp.where(slot < 3, 1.0, 0.0).astype(F32)
        parts = [high, ones, low, jnp.zeros_like(ones)]
        return jnp.concatenate(parts, axis=0).astype(BF16)

    def load(fields, fields_ref, operand_ref):
        body, end = fields[:split] * LOG2E, fields[split:]
        end = jnp.where(slots(end) == 7, end, end * LOG2E)
        fields_ref[0:split] = body
        fields_ref[split:FIELD_ROWS] = end
        operand_ref[...] = operand_of(body, end)

    def chunk_of(chunk):
        return jnp.concatenate([flat[row_of(chunk, row)] for row in range(CHUNK)], axis=1)

    def rates(operand_ref, net_ref):
        powers = jnp.dot(exponent_table[...], operand_ref[...], preferred_element_type=F32)
        count = powers.shape[1]
        powers = powers.reshape(laws // 8, 2, 8, count)
        net = jnp.exp2(powers[:, 0]) - jnp.exp2(powers[:, 1])
        high, low = split_pair(net)
        pieces = jnp.concatenate([high[:, None], low[:, None]], axis=1)
        net_ref[...] = pieces.reshape(2 * laws, count).astype(BF16)

    def advance(net_ref, fields_ref):
        change = jnp.dot(sum_table[...], net_ref[...], preferred_element_type=F32)
        end_change = change[split:FIELD_ROWS] + change[FIELD_ROWS:]
        body, end = fields_ref[0:split], fields_ref[split:FIELD_ROWS]
        slot = slots(end)
        step = end[7:8]
        gain = jnp.where(
            slot < species - split,
            jnp.exp2(-end),
            jnp.where(slot == species - split, 1.0, 0.0),
        )
        body = body + step * (change[:split] * jnp.exp2(-body))
        end = end + step * (end_change * gain)
        return body, end

    def renew(net_ref, fields_ref, operand_ref):
        body, end = advance(net_ref, fields_ref)
        fields_ref[0:split] = body
        fields_ref[split:FIELD_ROWS] = end
        operand_ref[...] = operand_of(body, end)

    def finish(chunk, body, end):
        fields = jnp.concatenate([body, end], axis=0) * LN2
        for row in range(CHUNK):
            flat[row_of(chunk, row)] = fields[:, row * width : (row + 1) * width]

    def collect(chunk):
        base = chunk * CHUNK
        first = jnp.zeros((FIELD_ROWS, width), F32)
        last = jnp.zeros((FIELD_ROWS, width), F32)
        for row in range(CHUNK):
            part = flat[row_of(chunk, row)]
            first = jnp.where(lane == row, pltpu.roll(part, row, 1), first)
            last = jnp.where(lane == row, pltpu.roll(part, row + 1, 1), last)
        mine = (lane >= base) & (lane < base + CHUNK)
        turn = base % width
        sides[0] = jnp.where(mine, pltpu.roll(first, turn, 1), sides[0])
        sides[1] = jnp.where(mine, pltpu.roll(last, turn, 1), sides[1])

    def arrive(chunk):
        for copy in fetches(chunk):
            copy.wait()

    arrive(0)
    collect(0)
    edges[DOWN] = flat[row_of(0, 0)]
    load(chunk_of(0), fields_a, operand_a)
    fields_b[...] = jnp.ones_like(fields_b)
    net_b[...] = jnp.zeros_like(net_b)
    pairs = chunks // 2
    gathered = chunks // AHEAD

    @pl.loop(0, pairs)
    def _(pair):
        a, b = 2 * pair, 2 * pair + 1

        @pl.when(pair == 0)
        def _():
            arrive(1)
            arrive(2)

        @pl.when(pair == 1)
        def _():
            @pl.loop(3, chunks)
            def _(chunk):
                arrive(chunk)

        @pl.when(pair == gathered + 1)
        def _():
            edges[RIGHT] = sides[0]
            edges[LEFT] = sides[1]
            edges[UP] = flat[row_of(chunks - 1, CHUNK - 1)]
            pl.semaphore_wait(barrier, 4)
            for copy in sends():
                copy.start()

        @pl.when(pair > 0)
        def _():
            flush(a - 2).start()

        @pl.when(pair > 1)
        def _():
            flush(b - 4).start()

        collects = (pair > 0) & (pair <= gathered)
        for index in range(AHEAD):
            collect(jnp.where(collects, (pair - 1) * AHEAD + 1 + index, chunks))

        for substep in range(SUBSTEPS):
            rates(operand_a, net_a)
            if substep == 0:
                finish(jnp.where(pair == 0, chunks, b - 2), *advance(net_b, fields_b))
                load(chunk_of(b), fields_b, operand_b)
            else:
                renew(net_b, fields_b, operand_b)
            rates(operand_b, net_b)
            if substep == SUBSTEPS - 1:
                finish(a, *advance(net_a, fields_a))
                load(chunk_of(jnp.minimum(a + 2, chunks - 1)), fields_a, operand_a)
            else:
                renew(net_a, fields_a, operand_a)

    flush(chunks - 3).start()
    flush(chunks - 2).start()
    for copy in sends():
        copy.wait()
    finish(chunks - 1, *advance(net_b, fields_b))
    count = 4 * width
    fields_h, operand_h, net_h = (
        ref.at[:, pl.ds(0, count)] for ref in (fields_a, operand_a, net_a)
    )
    load(jnp.concatenate([halos[place] for place in range(4)], axis=1), fields_h, operand_h)
    for _ in range(SUBSTEPS):
        rates(operand_h, net_h)
        renew(net_h, fields_h, operand_h)
    flush(chunks - 1).start()
    for place in range(4):
        edges[place] = fields_h[:, place * width : (place + 1) * width] * LN2
    copy = pltpu.make_async_copy(edges, halo_ref, halo_sem)
    copy.start()

    @pl.loop(0, chunks)
    def _(chunk):
        flush(chunk).wait()

    copy.wait()


def transport_kernel(
    state_ref,
    spread_input,
    halo_input,
    conc_ref,
    temp_ref,
    spread_ref,
    halo_ref,
    old,
    new,
    gains,
    sides,
    sheet,
    small_sem,
    in_sem,
    out_sem,
    temp_sem,
):
    species, rows, width = conc_ref.shape
    blocks = (species + 1) // BLOCK
    row = lax.broadcasted_iota(jnp.int32, (rows, width), 0)
    lane = lax.broadcasted_iota(jnp.int32, (rows, width), 1)

    def fetch(block):
        at = pl.ds(block * BLOCK, BLOCK)
        return pltpu.make_async_copy(state_ref.at[at], old.at[at], in_sem.at[block])

    def flush(block, count):
        at = pl.ds(block * BLOCK, count)
        return pltpu.make_async_copy(new.at[at], conc_ref.at[at], out_sem.at[block])

    def flush_temper():
        return pltpu.make_async_copy(new.at[species], temp_ref, temp_sem)

    smalls = [
        pltpu.make_async_copy(halo_input, halo_ref, small_sem.at[0]),
        pltpu.make_async_copy(spread_input, spread_ref, small_sem.at[1]),
    ]
    for copy in smalls:
        copy.start()

    @pl.loop(0, blocks)
    def _(block):
        fetch(block).start()

    for copy in smalls:
        copy.wait()

    def around(here, component):
        north = jnp.where(row == 0, halo_ref[UP, component], pltpu.roll(here, 1, 0))
        south = jnp.where(
            row == rows - 1, halo_ref[DOWN, component], pltpu.roll(here, rows - 1, 0)
        )
        side = pltpu.roll(sides[...], width - 1 - 2 * component, 1)
        west = jnp.where(lane == 0, side, pltpu.roll(here, 1, 1))
        east = jnp.where(lane == width - 1, side, pltpu.roll(here, width - 1, 1))
        return north, south, west, east

    sheet[...] = jnp.zeros_like(sheet)
    sheet[pl.ds(0, FIELD_ROWS, stride=2)] = halo_ref[RIGHT]
    sheet[pl.ds(1, FIELD_ROWS, stride=2)] = halo_ref[LEFT]
    sides[...] = sheet[...].T
    here = spread_ref[...]
    rest = jnp.ones_like(here)
    for index, near in enumerate(around(here, FIELD_ROWS - 2)):
        gain = (0.5 * DIFFUSION_NUMBER) * (here + near)
        gains[index] = gain
        rest = rest - gain
    gains[4] = rest

    @pl.loop(0, blocks)
    def _(block):
        fetch(block).wait()
        for index in range(BLOCK):
            component = block * BLOCK + index
            here = old[component]
            total = gains[4] * here
            for which, near in enumerate(around(here, component)):
                total = total + gains[which] * near
            new[component] = total

        @pl.when(block < blocks - 1)
        def _():
            flush(block, BLOCK).start()

    flush(blocks - 1, BLOCK - 1).start()
    flush_temper().start()

    @pl.loop(0, blocks - 1)
    def _(block):
        flush(block, BLOCK).wait()

    flush(blocks - 1, BLOCK - 1).wait()
    flush_temper().wait()


def per_device(
    molar_density_logs,
    scaled_thermal_state,
    spreading_rate,
    tile_burning_load,
    input_multipliers,
    output_multipliers,
    arrhenius_prefactor_logs,
    arrhenius_barrier,
    balance_ratio_logs,
    enthalpy_yield,
):
    rows, species, width = molar_density_logs.shape
    laws = input_multipliers.shape[0]
    padded = -(-laws // 8) * 8
    wide = -(-laws // 128) * 128
    chunks = rows // CHUNK
    cells = CHUNK * width
    anywhere = pl.BlockSpec(memory_space=pl.ANY)
    state, halo = pl.pallas_call(
        chemistry_kernel,
        out_shape=(
            jax.ShapeDtypeStruct((FIELD_ROWS, rows, width), F32),
            jax.ShapeDtypeStruct((4, FIELD_ROWS, width), F32),
        ),
        in_specs=[anywhere] * 10,
        out_specs=(anywhere,) * 2,
        scratch_shapes=[
            pltpu.VMEM((chunks + 1, FIELD_ROWS, CHUNK, width), F32),
            pltpu.VMEM((1, rows), jnp.int32),
            pltpu.VMEM((species, laws), jnp.int32),
            pltpu.VMEM((species, laws), jnp.int32),
            pltpu.VMEM((laws,), F32),
            pltpu.VMEM((laws,), F32),
            pltpu.VMEM((laws,), F32),
            pltpu.VMEM((laws,), F32),
            pltpu.VMEM((4, FIELD_ROWS, width), F32),
            pltpu.VMEM((4, FIELD_ROWS, width), F32),
            pltpu.VMEM((2, FIELD_ROWS, width), F32),
            pltpu.VMEM((2 * padded, 2 * SLOTS), BF16),
            pltpu.VMEM((SLOTS, 2 * padded), BF16),
            pltpu.VMEM((8, wide), F32),
            pltpu.VMEM((2 * SLOTS, wide), F32),
            pltpu.VMEM((FIELD_ROWS, cells), F32),
            pltpu.VMEM((FIELD_ROWS, cells), F32),
            pltpu.VMEM((2 * SLOTS, cells), BF16),
            pltpu.VMEM((2 * SLOTS, cells), BF16),
            pltpu.VMEM((2 * padded, cells), BF16),
            pltpu.VMEM((2 * padded, cells), BF16),
            pltpu.SemaphoreType.DMA((7,)),
            pltpu.SemaphoreType.DMA((3, chunks)),
            pltpu.SemaphoreType.DMA((chunks,)),
            pltpu.SemaphoreType.DMA(()),
            pltpu.SemaphoreType.DMA((4,)),
            pltpu.SemaphoreType.DMA((4,)),
        ],
        compiler_params=pltpu.CompilerParams(
            collective_id=0, has_side_effects=True, vmem_limit_bytes=60 * 2**20
        ),
        name="chemistry",
    )(
        jnp.transpose(molar_density_logs, (1, 0, 2)),
        scaled_thermal_state,
        spreading_rate,
        tile_burning_load.reshape(1, rows),
        input_multipliers.T,
        output_multipliers.T,
        arrhenius_prefactor_logs,
        arrhenius_barrier,
        balance_ratio_logs,
        enthalpy_yield,
    )

    blocks = (species + 1) // BLOCK
    conc, temp = pl.pallas_call(
        transport_kernel,
        out_shape=(
            jax.ShapeDtypeStruct((species, rows, width), F32),
            jax.ShapeDtypeStruct((rows, width), F32),
        ),
        in_specs=[anywhere] * 3,
        out_specs=(anywhere, anywhere),
        scratch_shapes=[
            pltpu.VMEM((rows, width), F32),
            pltpu.VMEM((4, FIELD_ROWS, width), F32),
            pltpu.VMEM((species + 1, rows, width), F32),
            pltpu.VMEM((species + 1, rows, width), F32),
            pltpu.VMEM((5, rows, width), F32),
            pltpu.VMEM((rows, width), F32),
            pltpu.VMEM((width, rows), F32),
            pltpu.SemaphoreType.DMA((2,)),
            pltpu.SemaphoreType.DMA((blocks,)),
            pltpu.SemaphoreType.DMA((blocks,)),
            pltpu.SemaphoreType.DMA(()),
        ],
        compiler_params=pltpu.CompilerParams(vmem_limit_bytes=60 * 2**20),
        name="transport",
    )(state, spreading_rate, halo)
    return jnp.transpose(conc, (1, 0, 2)), temp


def solution(mesh):
    placed = (
        P("gx", None, "gy"),
        P("gx", "gy"),
        P("gx", "gy"),
        P("gx", "gy"),
        P(),
        P(),
        P(),
        P(),
        P(),
        P(),
    )
    return jax.shard_map(
        per_device,
        mesh=mesh,
        in_specs=placed,
        out_specs=(P("gx", None, "gy"), P("gx", "gy")),
        check_vma=False,
    )
```

```python
import jax
import jax.numpy as jnp
from jax import lax
from jax.experimental import pallas as pl
from jax.experimental.pallas import tpu as pltpu
from jax.sharding import PartitionSpec as P

SUBSTEPS = 4
TIME_STEP = 0.01
DIFFUSION_NUMBER = 0.1
LOG2E = 1.4426950408889634
LN2 = 0.6931471805599453

TILE = 8
CHUNK = 16
AHEAD = 4
SLOTS = 64
FIELD_ROWS = 56
BLOCK = 6
UP, DOWN, LEFT, RIGHT = range(4)

BF16 = jnp.bfloat16
F32 = jnp.float32


def split_pair(x):
    high = x.astype(BF16).astype(F32)
    return high, x - high


def split_three(x):
    first = x.astype(BF16).astype(F32)
    rest = x - first
    second = rest.astype(BF16).astype(F32)
    return first, second, rest - second


def fill_tables(
    forward_ref, backward_ref, law_refs, exponent_table, sum_table, line, stage
):
    species, laws = forward_ref.shape
    total = exponent_table.shape[0]
    padded = total // 2
    wide = stage.shape[1]
    stage[...] = jnp.zeros_like(stage)
    line[...] = jnp.zeros_like(line)
    for index, ref in enumerate(law_refs):
        line[index : index + 1, 0:laws] = ref[...].reshape(1, laws)
    prefactor, barrier, balance, heat = (line[index : index + 1] for index in range(4))
    b1, b2, b3 = split_three((-LOG2E * LOG2E) * barrier)

    def table(table_ref, constant):
        stage[0:species, 0:laws] = table_ref[...].astype(F32)
        stage[SLOTS : SLOTS + species, 0:laws] = table_ref[...].astype(F32)
        for index, piece in enumerate((b1, b2, b3) + split_three(LOG2E * constant)):
            stage[species + index : species + index + 1] = piece
        for index, piece in enumerate((b1, b2)):
            at = SLOTS + species + index
            stage[at : at + 1] = piece
        return stage[...].T[:padded]

    first = table(forward_ref, prefactor)
    second = table(backward_ref, prefactor - balance)
    pairs = [half.reshape(padded // 8, 1, 8, 2 * SLOTS) for half in (first, second)]
    pairs = jnp.concatenate(pairs, axis=1).reshape(total, 2 * SLOTS)
    exponent_table[...] = pairs.astype(BF16)

    stage[...] = jnp.zeros_like(stage)
    stage[0:species, 0:laws] = (backward_ref[...] - forward_ref[...]).astype(F32)
    high, low = split_pair(heat)
    stage[species : species + 1] = high
    stage[species + 8 : species + 9] = low
    law = lax.broadcasted_iota(jnp.int32, (wide, total), 0)
    place = lax.broadcasted_iota(jnp.int32, (wide, total), 1)
    chosen = jnp.where(law == (place // 16) * 8 + place % 8, 1.0, 0.0).astype(BF16)
    spread = jnp.dot(stage[0:SLOTS].astype(BF16), chosen, preferred_element_type=F32)
    sum_table[...] = spread.astype(BF16)


def chemistry_kernel(
    logs_ref,
    temper_ref,
    spread_ref,
    load_input,
    forward_input,
    backward_input,
    prefactor_input,
    barrier_input,
    balance_input,
    heat_input,
    state_ref,
    halo_ref,
    cells_ref,
    load_ref,
    forward_ref,
    backward_ref,
    prefactor_ref,
    barrier_ref,
    balance_ref,
    heat_ref,
    edges,
    halos,
    sides,
    exponent_table,
    sum_table,
    line,
    stage,
    fields_a,
    fields_b,
    operand_a,
    operand_b,
    net_a,
    net_b,
    small_sem,
    plane_sem,
    in_sem,
    out_sem,
    halo_sem,
    send_sem,
    recv_sem,
):
    species, rows, width = logs_ref.shape
    tiles, chunks = rows // TILE, rows // CHUNK
    share = CHUNK // TILE
    cells = CHUNK * width
    laws = exponent_table.shape[0] // 2
    gx, gy = lax.axis_index("gx"), lax.axis_index("gy")
    nx, ny = lax.axis_size("gx"), lax.axis_size("gy")
    up = (lax.rem(gx + nx - 1, nx), gy)
    down = (lax.rem(gx + 1, nx), gy)
    left = (gx, lax.rem(gy + ny - 1, ny))
    right = (gx, lax.rem(gy + 1, ny))

    def fetch(tile):
        at = pl.ds(pl.multiple_of(tile * TILE, TILE), TILE)
        target = cells_ref.at[tile, pl.ds(0, species)]
        return pltpu.make_async_copy(logs_ref.at[:, at], target, in_sem.at[tile])

    def spread_out(plane_ref, place, sem):
        target = cells_ref.at[pl.ds(0, tiles), place]
        return pltpu.make_async_copy(plane_ref.reshape(tiles, TILE, width), target, sem)

    def flush(tile):
        at = pl.ds(pl.multiple_of(tile * TILE, TILE), TILE)
        return pltpu.make_async_copy(cells_ref.at[tile], state_ref.at[:, at], out_sem.at[tile])

    def leave(chunk):
        for index in range(share):
            flush(chunk * share + index).start()

    def sends():
        copies = []
        for place, device in ((UP, down), (DOWN, up), (LEFT, right), (RIGHT, left)):
            copies.append(
                pltpu.make_async_remote_copy(
                    src_ref=edges.at[place],
                    dst_ref=halos.at[place],
                    send_sem=send_sem.at[place],
                    recv_sem=recv_sem.at[place],
                    device_id=device,
                    device_id_type=pl.DeviceIdType.MESH,
                )
            )
        return copies

    pairs_of = (
        (load_input, load_ref),
        (forward_input, forward_ref),
        (backward_input, backward_ref),
        (prefactor_input, prefactor_ref),
        (barrier_input, barrier_ref),
        (balance_input, balance_ref),
        (heat_input, heat_ref),
    )
    smalls = [
        pltpu.make_async_copy(source, target, small_sem.at[index])
        for index, (source, target) in enumerate(pairs_of)
    ]
    smalls.append(spread_out(temper_ref, species, plane_sem.at[0]))
    smalls.append(spread_out(spread_ref, species + 1, plane_sem.at[1]))
    fetch(0).start()
    for copy in smalls:
        copy.start()

    @pl.loop(1, tiles)
    def _(tile):
        fetch(tile).start()

    barrier = pltpu.get_barrier_semaphore()
    for neighbour in (up, down, left, right):
        pl.semaphore_signal(
            barrier, inc=1, device_id=neighbour, device_id_type=pl.DeviceIdType.MESH
        )

    for copy in smalls:
        copy.wait()
    steps = jnp.where(load_ref[...] > 0, TIME_STEP * LOG2E, 0.0).astype(F32)
    steps = jnp.broadcast_to(steps, (rows, width)).T
    for tile in range(tiles):
        cells_ref[tile, species + 2] = steps[tile * TILE : (tile + 1) * TILE]
    fill_tables(
        forward_ref,
        backward_ref,
        (prefactor_ref, barrier_ref, balance_ref, heat_ref),
        exponent_table,
        sum_table,
        line,
        stage,
    )

    sides[...] = jnp.zeros_like(sides)
    cells_ref[tiles:] = jnp.zeros((share,) + cells_ref.shape[1:], F32)
    split = FIELD_ROWS - 8
    lane = lax.broadcasted_iota(jnp.int32, (FIELD_ROWS, width), 1)
    flat = cells_ref.reshape((tiles + share) * FIELD_ROWS * TILE, width)

    def row_of(chunk, row):
        tile = chunk * share + row // TILE
        return pl.ds(tile * (FIELD_ROWS * TILE) + row % TILE, FIELD_ROWS, stride=TILE)

    def slots(like):
        return lax.broadcasted_iota(jnp.int32, (8, like.shape[1]), 0)

    def operand_of(body, end):
        slot = slots(end)
        inverse = 1.0 / end[species - split : species - split + 1]
        inverse = jnp.broadcast_to(inverse, end.shape)
        end = jnp.where(slot < species - split, end, inverse)
        high, low = split_pair(jnp.concatenate([body, end], axis=0))
        ones = jnp.where(slot < 3, 1.0, 0.0).astype(F32)
        parts = [high, ones, low, jnp.zeros_like(ones)]
        return jnp.concatenate(parts, axis=0).astype(BF16)

    def load(fields, fields_ref, operand_ref):
        body, end = fields[:split] * LOG2E, fields[split:]
        end = jnp.where(slots(end) == 7, end, end * LOG2E)
        fields_ref[0:split] = body
        fields_ref[split:FIELD_ROWS] = end
        operand_ref[...] = operand_of(body, end)

    def chunk_of(chunk):
        return jnp.concatenate([flat[row_of(chunk, row)] for row in range(CHUNK)], axis=1)

    def rates(operand_ref, net_ref):
        powers = jnp.dot(exponent_table[...], operand_ref[...], preferred_element_type=F32)
        count = powers.shape[1]
        powers = powers.reshape(laws // 8, 2, 8, count)
        net = jnp.exp2(powers[:, 0]) - jnp.exp2(powers[:, 1])
        high, low = split_pair(net)
        pieces = jnp.concatenate([high[:, None], low[:, None]], axis=1)
        net_ref[...] = pieces.reshape(2 * laws, count).astype(BF16)

    def advance(net_ref, fields_ref):
        change = jnp.dot(sum_table[...], net_ref[...], preferred_element_type=F32)
        end_change = change[split:FIELD_ROWS] + change[FIELD_ROWS:]
        body, end = fields_ref[0:split], fields_ref[split:FIELD_ROWS]
        slot = slots(end)
        step = end[7:8]
        gain = jnp.where(
            slot < species - split,
            jnp.exp2(-end),
            jnp.where(slot == species - split, 1.0, 0.0),
        )
        body = body + step * (change[:split] * jnp.exp2(-body))
        end = end + step * (end_change * gain)
        return body, end

    def renew(net_ref, fields_ref, operand_ref):
        body, end = advance(net_ref, fields_ref)
        fields_ref[0:split] = body
        fields_ref[split:FIELD_ROWS] = end
        operand_ref[...] = operand_of(body, end)

    def finish(chunk, body, end):
        fields = jnp.concatenate([body, end], axis=0) * LN2
        for row in range(CHUNK):
            flat[row_of(chunk, row)] = fields[:, row * width : (row + 1) * width]

    def collect(chunk):
        base = chunk * CHUNK
        first = jnp.zeros((FIELD_ROWS, width), F32)
        last = jnp.zeros((FIELD_ROWS, width), F32)
        for row in range(CHUNK):
            part = flat[row_of(chunk, row)]
            first = jnp.where(lane == row, pltpu.roll(part, row, 1), first)
            last = jnp.where(lane == row, pltpu.roll(part, row + 1, 1), last)
        mine = (lane >= base) & (lane < base + CHUNK)
        turn = base % width
        sides[0] = jnp.where(mine, pltpu.roll(first, turn, 1), sides[0])
        sides[1] = jnp.where(mine, pltpu.roll(last, turn, 1), sides[1])

    for tile in range(share):
        fetch(tile).wait()
    collect(0)
    edges[DOWN] = flat[row_of(0, 0)]
    load(chunk_of(0), fields_a, operand_a)
    fields_b[...] = jnp.ones_like(fields_b)
    net_b[...] = jnp.zeros_like(net_b)
    pairs = chunks // 2
    gathered = chunks // AHEAD

    @pl.loop(0, pairs)
    def _(pair):
        a, b = 2 * pair, 2 * pair + 1

        @pl.when(pair == 0)
        def _():
            for tile in range(share, 3 * share):
                fetch(tile).wait()

        @pl.when(pair == 1)
        def _():
            @pl.loop(3 * share, tiles)
            def _(tile):
                fetch(tile).wait()

        @pl.when(pair == gathered + 1)
        def _():
            edges[RIGHT] = sides[0]
            edges[LEFT] = sides[1]
            edges[UP] = flat[row_of(chunks - 1, CHUNK - 1)]
            pl.semaphore_wait(barrier, 4)
            for copy in sends():
                copy.start()

        @pl.when(pair > 0)
        def _():
            leave(a - 2)

        @pl.when(pair > 1)
        def _():
            leave(b - 4)

        collects = (pair > 0) & (pair <= gathered)
        for index in range(AHEAD):
            collect(jnp.where(collects, (pair - 1) * AHEAD + 1 + index, chunks))

        for substep in range(SUBSTEPS):
            rates(operand_a, net_a)
            if substep == 0:
                finish(jnp.where(pair == 0, chunks, b - 2), *advance(net_b, fields_b))
                load(chunk_of(b), fields_b, operand_b)
            else:
                renew(net_b, fields_b, operand_b)
            rates(operand_b, net_b)
            if substep == SUBSTEPS - 1:
                finish(a, *advance(net_a, fields_a))
                load(chunk_of(jnp.minimum(a + 2, chunks - 1)), fields_a, operand_a)
            else:
                renew(net_a, fields_a, operand_a)

    leave(chunks - 3)
    leave(chunks - 2)
    for copy in sends():
        copy.wait()
    finish(chunks - 1, *advance(net_b, fields_b))
    count = 4 * width
    fields_h, operand_h, net_h = (
        ref.at[:, pl.ds(0, count)] for ref in (fields_a, operand_a, net_a)
    )
    load(jnp.concatenate([halos[place] for place in range(4)], axis=1), fields_h, operand_h)
    for _ in range(SUBSTEPS):
        rates(operand_h, net_h)
        renew(net_h, fields_h, operand_h)
    leave(chunks - 1)
    for place in range(4):
        edges[place] = fields_h[:, place * width : (place + 1) * width] * LN2
    copy = pltpu.make_async_copy(edges, halo_ref, halo_sem)
    copy.start()

    @pl.loop(0, tiles)
    def _(tile):
        flush(tile).wait()

    copy.wait()


def transport_kernel(
    state_ref,
    spread_input,
    halo_input,
    conc_ref,
    temp_ref,
    spread_ref,
    halo_ref,
    old,
    new,
    gains,
    sides,
    sheet,
    small_sem,
    in_sem,
    out_sem,
    temp_sem,
):
    species, rows, width = conc_ref.shape
    blocks = (species + 1) // BLOCK
    row = lax.broadcasted_iota(jnp.int32, (rows, width), 0)
    lane = lax.broadcasted_iota(jnp.int32, (rows, width), 1)

    def fetch(block):
        at = pl.ds(block * BLOCK, BLOCK)
        return pltpu.make_async_copy(state_ref.at[at], old.at[at], in_sem.at[block])

    def flush(block, count):
        at = pl.ds(block * BLOCK, count)
        return pltpu.make_async_copy(new.at[at], conc_ref.at[at], out_sem.at[block])

    def flush_temper():
        return pltpu.make_async_copy(new.at[species], temp_ref, temp_sem)

    smalls = [
        pltpu.make_async_copy(halo_input, halo_ref, small_sem.at[0]),
        pltpu.make_async_copy(spread_input, spread_ref, small_sem.at[1]),
    ]
    for copy in smalls:
        copy.start()

    @pl.loop(0, blocks)
    def _(block):
        fetch(block).start()

    for copy in smalls:
        copy.wait()

    def around(here, component):
        north = jnp.where(row == 0, halo_ref[UP, component], pltpu.roll(here, 1, 0))
        south = jnp.where(
            row == rows - 1, halo_ref[DOWN, component], pltpu.roll(here, rows - 1, 0)
        )
        side = pltpu.roll(sides[...], width - 1 - 2 * component, 1)
        west = jnp.where(lane == 0, side, pltpu.roll(here, 1, 1))
        east = jnp.where(lane == width - 1, side, pltpu.roll(here, width - 1, 1))
        return north, south, west, east

    sheet[...] = jnp.zeros_like(sheet)
    sheet[pl.ds(0, FIELD_ROWS, stride=2)] = halo_ref[RIGHT]
    sheet[pl.ds(1, FIELD_ROWS, stride=2)] = halo_ref[LEFT]
    sides[...] = sheet[...].T
    here = spread_ref[...]
    rest = jnp.ones_like(here)
    for index, near in enumerate(around(here, FIELD_ROWS - 2)):
        gain = (0.5 * DIFFUSION_NUMBER) * (here + near)
        gains[index] = gain
        rest = rest - gain
    gains[4] = rest

    @pl.loop(0, blocks)
    def _(block):
        fetch(block).wait()
        for index in range(BLOCK):
            component = block * BLOCK + index
            here = old[component]
            total = gains[4] * here
            for which, near in enumerate(around(here, component)):
                total = total + gains[which] * near
            new[component] = total

        @pl.when(block < blocks - 1)
        def _():
            flush(block, BLOCK).start()

    flush(blocks - 1, BLOCK - 1).start()
    flush_temper().start()

    @pl.loop(0, blocks - 1)
    def _(block):
        flush(block, BLOCK).wait()

    flush(blocks - 1, BLOCK - 1).wait()
    flush_temper().wait()


def per_device(
    molar_density_logs,
    scaled_thermal_state,
    spreading_rate,
    tile_burning_load,
    input_multipliers,
    output_multipliers,
    arrhenius_prefactor_logs,
    arrhenius_barrier,
    balance_ratio_logs,
    enthalpy_yield,
):
    rows, species, width = molar_density_logs.shape
    laws = input_multipliers.shape[0]
    padded = -(-laws // 8) * 8
    wide = -(-laws // 128) * 128
    tiles = rows // TILE
    cells = CHUNK * width
    anywhere = pl.BlockSpec(memory_space=pl.ANY)
    state, halo = pl.pallas_call(
        chemistry_kernel,
        out_shape=(
            jax.ShapeDtypeStruct((FIELD_ROWS, rows, width), F32),
            jax.ShapeDtypeStruct((4, FIELD_ROWS, width), F32),
        ),
        in_specs=[anywhere] * 10,
        out_specs=(anywhere,) * 2,
        scratch_shapes=[
            pltpu.VMEM((tiles + CHUNK // TILE, FIELD_ROWS, TILE, width), F32),
            pltpu.VMEM((1, rows), jnp.int32),
            pltpu.VMEM((species, laws), jnp.int32),
            pltpu.VMEM((species, laws), jnp.int32),
            pltpu.VMEM((laws,), F32),
            pltpu.VMEM((laws,), F32),
            pltpu.VMEM((laws,), F32),
            pltpu.VMEM((laws,), F32),
            pltpu.VMEM((4, FIELD_ROWS, width), F32),
            pltpu.VMEM((4, FIELD_ROWS, width), F32),
            pltpu.VMEM((2, FIELD_ROWS, width), F32),
            pltpu.VMEM((2 * padded, 2 * SLOTS), BF16),
            pltpu.VMEM((SLOTS, 2 * padded), BF16),
            pltpu.VMEM((8, wide), F32),
            pltpu.VMEM((2 * SLOTS, wide), F32),
            pltpu.VMEM((FIELD_ROWS, cells), F32),
            pltpu.VMEM((FIELD_ROWS, cells), F32),
            pltpu.VMEM((2 * SLOTS, cells), BF16),
            pltpu.VMEM((2 * SLOTS, cells), BF16),
            pltpu.VMEM((2 * padded, cells), BF16),
            pltpu.VMEM((2 * padded, cells), BF16),
            pltpu.SemaphoreType.DMA((7,)),
            pltpu.SemaphoreType.DMA((2,)),
            pltpu.SemaphoreType.DMA((tiles,)),
            pltpu.SemaphoreType.DMA((tiles,)),
            pltpu.SemaphoreType.DMA(()),
            pltpu.SemaphoreType.DMA((4,)),
            pltpu.SemaphoreType.DMA((4,)),
        ],
        compiler_params=pltpu.CompilerParams(
            collective_id=0, has_side_effects=True, vmem_limit_bytes=60 * 2**20
        ),
        name="chemistry",
    )(
        jnp.transpose(molar_density_logs, (1, 0, 2)),
        scaled_thermal_state,
        spreading_rate,
        tile_burning_load.reshape(1, rows),
        input_multipliers.T,
        output_multipliers.T,
        arrhenius_prefactor_logs,
        arrhenius_barrier,
        balance_ratio_logs,
        enthalpy_yield,
    )

    blocks = (species + 1) // BLOCK
    conc, temp = pl.pallas_call(
        transport_kernel,
        out_shape=(
            jax.ShapeDtypeStruct((species, rows, width), F32),
            jax.ShapeDtypeStruct((rows, width), F32),
        ),
        in_specs=[anywhere] * 3,
        out_specs=(anywhere, anywhere),
        scratch_shapes=[
            pltpu.VMEM((rows, width), F32),
            pltpu.VMEM((4, FIELD_ROWS, width), F32),
            pltpu.VMEM((species + 1, rows, width), F32),
            pltpu.VMEM((species + 1, rows, width), F32),
            pltpu.VMEM((5, rows, width), F32),
            pltpu.VMEM((rows, width), F32),
            pltpu.VMEM((width, rows), F32),
            pltpu.SemaphoreType.DMA((2,)),
            pltpu.SemaphoreType.DMA((blocks,)),
            pltpu.SemaphoreType.DMA((blocks,)),
            pltpu.SemaphoreType.DMA(()),
        ],
        compiler_params=pltpu.CompilerParams(vmem_limit_bytes=60 * 2**20),
        name="transport",
    )(state, spreading_rate, halo)
    return jnp.transpose(conc, (1, 0, 2)), temp


def solution(mesh):
    placed = (
        P("gx", None, "gy"),
        P("gx", "gy"),
        P("gx", "gy"),
        P("gx", "gy"),
        P(),
        P(),
        P(),
        P(),
        P(),
        P(),
    )
    return jax.shard_map(
        per_device,
        mesh=mesh,
        in_specs=placed,
        out_specs=(P("gx", None, "gy"), P("gx", "gy")),
        check_vma=False,
    )
```

```python
import jax
import jax.numpy as jnp
from jax import lax
from jax.experimental import pallas as pl
from jax.experimental.pallas import tpu as pltpu
from jax.sharding import PartitionSpec as P

SUBSTEPS = 4
TIME_STEP = 0.01
DIFFUSION_NUMBER = 0.1
LOG2E = 1.4426950408889634
LN2 = 0.6931471805599453

TILE = 8
CHUNK = 16
AHEAD = 3
SLOTS = 64
FIELD_ROWS = 56
BLOCK = 6
UP, DOWN, LEFT, RIGHT = range(4)

BF16 = jnp.bfloat16
F32 = jnp.float32


def split_pair(x):
    high = x.astype(BF16).astype(F32)
    return high, x - high


def split_three(x):
    first = x.astype(BF16).astype(F32)
    rest = x - first
    second = rest.astype(BF16).astype(F32)
    return first, second, rest - second


def fill_tables(
    forward_ref, backward_ref, law_refs, exponent_table, sum_table, line, stage
):
    species, laws = forward_ref.shape
    total = exponent_table.shape[0]
    padded = total // 2
    wide = stage.shape[1]
    stage[...] = jnp.zeros_like(stage)
    line[...] = jnp.zeros_like(line)
    for index, ref in enumerate(law_refs):
        line[index : index + 1, 0:laws] = ref[...].reshape(1, laws)
    prefactor, barrier, balance, heat = (line[index : index + 1] for index in range(4))
    b1, b2, b3 = split_three((-LOG2E * LOG2E) * barrier)

    def table(table_ref, constant):
        stage[0:species, 0:laws] = table_ref[...].astype(F32)
        stage[SLOTS : SLOTS + species, 0:laws] = table_ref[...].astype(F32)
        for index, piece in enumerate((b1, b2, b3) + split_three(LOG2E * constant)):
            stage[species + index : species + index + 1] = piece
        for index, piece in enumerate((b1, b2)):
            at = SLOTS + species + index
            stage[at : at + 1] = piece
        return stage[...].T[:padded]

    first = table(forward_ref, prefactor)
    second = table(backward_ref, prefactor - balance)
    pairs = [half.reshape(padded // 8, 1, 8, 2 * SLOTS) for half in (first, second)]
    pairs = jnp.concatenate(pairs, axis=1).reshape(total, 2 * SLOTS)
    exponent_table[...] = pairs.astype(BF16)

    stage[...] = jnp.zeros_like(stage)
    stage[0:species, 0:laws] = (backward_ref[...] - forward_ref[...]).astype(F32)
    high, low = split_pair(heat)
    stage[species : species + 1] = high
    stage[species + 8 : species + 9] = low
    law = lax.broadcasted_iota(jnp.int32, (wide, total), 0)
    place = lax.broadcasted_iota(jnp.int32, (wide, total), 1)
    chosen = jnp.where(law == (place // 16) * 8 + place % 8, 1.0, 0.0).astype(BF16)
    spread = jnp.dot(stage[0:SLOTS].astype(BF16), chosen, preferred_element_type=F32)
    sum_table[...] = spread.astype(BF16)


def chemistry_kernel(
    logs_ref,
    temper_ref,
    spread_ref,
    load_input,
    forward_input,
    backward_input,
    prefactor_input,
    barrier_input,
    balance_input,
    heat_input,
    state_ref,
    halo_ref,
    cells_ref,
    load_ref,
    forward_ref,
    backward_ref,
    prefactor_ref,
    barrier_ref,
    balance_ref,
    heat_ref,
    edges,
    halos,
    sides,
    exponent_table,
    sum_table,
    line,
    stage,
    fields_a,
    fields_b,
    operand_a,
    operand_b,
    net_a,
    net_b,
    small_sem,
    plane_sem,
    in_sem,
    out_sem,
    halo_sem,
    send_sem,
    recv_sem,
):
    species, rows, width = logs_ref.shape
    tiles, chunks = rows // TILE, rows // CHUNK
    share = CHUNK // TILE
    cells = CHUNK * width
    laws = exponent_table.shape[0] // 2
    gx, gy = lax.axis_index("gx"), lax.axis_index("gy")
    nx, ny = lax.axis_size("gx"), lax.axis_size("gy")
    up = (lax.rem(gx + nx - 1, nx), gy)
    down = (lax.rem(gx + 1, nx), gy)
    left = (gx, lax.rem(gy + ny - 1, ny))
    right = (gx, lax.rem(gy + 1, ny))

    def fetch(tile):
        at = pl.ds(pl.multiple_of(tile * TILE, TILE), TILE)
        target = cells_ref.at[tile, pl.ds(0, species)]
        return pltpu.make_async_copy(logs_ref.at[:, at], target, in_sem.at[tile])

    def spread_out(plane_ref, place, sem):
        target = cells_ref.at[pl.ds(0, tiles), place]
        return pltpu.make_async_copy(plane_ref.reshape(tiles, TILE, width), target, sem)

    def flush(tile):
        at = pl.ds(pl.multiple_of(tile * TILE, TILE), TILE)
        return pltpu.make_async_copy(cells_ref.at[tile], state_ref.at[:, at], out_sem.at[tile])

    def leave(chunk):
        for index in range(share):
            flush(chunk * share + index).start()

    def sends():
        copies = []
        for place, device in ((UP, down), (DOWN, up), (LEFT, right), (RIGHT, left)):
            copies.append(
                pltpu.make_async_remote_copy(
                    src_ref=edges.at[place],
                    dst_ref=halos.at[place],
                    send_sem=send_sem.at[place],
                    recv_sem=recv_sem.at[place],
                    device_id=device,
                    device_id_type=pl.DeviceIdType.MESH,
                )
            )
        return copies

    pairs_of = (
        (load_input, load_ref),
        (forward_input, forward_ref),
        (backward_input, backward_ref),
        (prefactor_input, prefactor_ref),
        (barrier_input, barrier_ref),
        (balance_input, balance_ref),
        (heat_input, heat_ref),
    )
    smalls = [
        pltpu.make_async_copy(source, target, small_sem.at[index])
        for index, (source, target) in enumerate(pairs_of)
    ]
    smalls.append(spread_out(temper_ref, species, plane_sem.at[0]))
    smalls.append(spread_out(spread_ref, species + 1, plane_sem.at[1]))
    fetch(0).start()
    for copy in smalls:
        copy.start()

    @pl.loop(1, tiles)
    def _(tile):
        fetch(tile).start()

    barrier = pltpu.get_barrier_semaphore()
    for neighbour in (up, down, left, right):
        pl.semaphore_signal(
            barrier, inc=1, device_id=neighbour, device_id_type=pl.DeviceIdType.MESH
        )

    for copy in smalls:
        copy.wait()
    steps = jnp.where(load_ref[...] > 0, TIME_STEP * LOG2E, 0.0).astype(F32)
    steps = jnp.broadcast_to(steps, (rows, width)).T
    for tile in range(tiles):
        cells_ref[tile, species + 2] = steps[tile * TILE : (tile + 1) * TILE]
    fill_tables(
        forward_ref,
        backward_ref,
        (prefactor_ref, barrier_ref, balance_ref, heat_ref),
        exponent_table,
        sum_table,
        line,
        stage,
    )

    sides[...] = jnp.zeros_like(sides)
    cells_ref[tiles:] = jnp.zeros((share,) + cells_ref.shape[1:], F32)
    split = FIELD_ROWS - 8
    lane = lax.broadcasted_iota(jnp.int32, (FIELD_ROWS, width), 1)
    flat = cells_ref.reshape((tiles + share) * FIELD_ROWS * TILE, width)

    def row_of(chunk, row):
        tile = chunk * share + row // TILE
        return pl.ds(tile * (FIELD_ROWS * TILE) + row % TILE, FIELD_ROWS, stride=TILE)

    def slots(like):
        return lax.broadcasted_iota(jnp.int32, (8, like.shape[1]), 0)

    def operand_of(body, end):
        slot = slots(end)
        inverse = 1.0 / end[species - split : species - split + 1]
        inverse = jnp.broadcast_to(inverse, end.shape)
        end = jnp.where(slot < species - split, end, inverse)
        high, low = split_pair(jnp.concatenate([body, end], axis=0))
        ones = jnp.where(slot < 3, 1.0, 0.0).astype(F32)
        parts = [high, ones, low, jnp.zeros_like(ones)]
        return jnp.concatenate(parts, axis=0).astype(BF16)

    def load(fields, fields_ref, operand_ref):
        body, end = fields[:split] * LOG2E, fields[split:]
        end = jnp.where(slots(end) == 7, end, end * LOG2E)
        fields_ref[0:split] = body
        fields_ref[split:FIELD_ROWS] = end
        operand_ref[...] = operand_of(body, end)

    def chunk_of(chunk):
        return jnp.concatenate([flat[row_of(chunk, row)] for row in range(CHUNK)], axis=1)

    def rates(operand_ref, net_ref):
        powers = jnp.dot(exponent_table[...], operand_ref[...], preferred_element_type=F32)
        count = powers.shape[1]
        powers = powers.reshape(laws // 8, 2, 8, count)
        net = jnp.exp2(powers[:, 0]) - jnp.exp2(powers[:, 1])
        high, low = split_pair(net)
        pieces = jnp.concatenate([high[:, None], low[:, None]], axis=1)
        net_ref[...] = pieces.reshape(2 * laws, count).astype(BF16)

    def advance(net_ref, fields_ref):
        change = jnp.dot(sum_table[...], net_ref[...], preferred_element_type=F32)
        end_change = change[split:FIELD_ROWS] + change[FIELD_ROWS:]
        body, end = fields_ref[0:split], fields_ref[split:FIELD_ROWS]
        slot = slots(end)
        step = end[7:8]
        gain = jnp.where(
            slot < species - split,
            jnp.exp2(-end),
            jnp.where(slot == species - split, 1.0, 0.0),
        )
        body = body + step * (change[:split] * jnp.exp2(-body))
        end = end + step * (end_change * gain)
        return body, end

    def renew(net_ref, fields_ref, operand_ref):
        body, end = advance(net_ref, fields_ref)
        fields_ref[0:split] = body
        fields_ref[split:FIELD_ROWS] = end
        operand_ref[...] = operand_of(body, end)

    def finish(chunk, body, end):
        fields = jnp.concatenate([body, end], axis=0) * LN2
        for row in range(CHUNK):
            flat[row_of(chunk, row)] = fields[:, row * width : (row + 1) * width]

    def collect(chunk):
        base = chunk * CHUNK
        first = jnp.zeros((FIELD_ROWS, width), F32)
        last = jnp.zeros((FIELD_ROWS, width), F32)
        for row in range(CHUNK):
            part = flat[row_of(chunk, row)]
            first = jnp.where(lane == row, pltpu.roll(part, row, 1), first)
            last = jnp.where(lane == row, pltpu.roll(part, row + 1, 1), last)
        mine = (lane >= base) & (lane < base + CHUNK)
        turn = base % width
        sides[0] = jnp.where(mine, pltpu.roll(first, turn, 1), sides[0])
        sides[1] = jnp.where(mine, pltpu.roll(last, turn, 1), sides[1])

    for tile in range(share):
        fetch(tile).wait()
    edges[DOWN] = flat[row_of(0, 0)]
    load(chunk_of(0), fields_a, operand_a)
    fields_b[...] = jnp.ones_like(fields_b)
    net_b[...] = jnp.zeros_like(net_b)
    pairs = chunks // 2
    gathered = -(-chunks // AHEAD)

    @pl.loop(0, pairs)
    def _(pair):
        a, b = 2 * pair, 2 * pair + 1

        @pl.when(pair == 0)
        def _():
            for tile in range(share, 3 * share):
                fetch(tile).wait()

        @pl.when(pair == 1)
        def _():
            @pl.loop(3 * share, tiles)
            def _(tile):
                fetch(tile).wait()

        @pl.when(pair == gathered)
        def _():
            edges[RIGHT] = sides[0]
            edges[LEFT] = sides[1]
            edges[UP] = flat[row_of(chunks - 1, CHUNK - 1)]
            pl.semaphore_wait(barrier, 4)
            for copy in sends():
                copy.start()

        @pl.when(pair > 0)
        def _():
            leave(a - 2)

        @pl.when(pair > 1)
        def _():
            leave(b - 4)

        for substep in range(SUBSTEPS):
            rates(operand_a, net_a)
            if substep == 0:
                finish(jnp.where(pair == 0, chunks, b - 2), *advance(net_b, fields_b))
                load(chunk_of(b), fields_b, operand_b)
            else:
                renew(net_b, fields_b, operand_b)
                collect(jnp.minimum(pair * AHEAD + substep - 1, chunks))
            rates(operand_b, net_b)
            if substep == SUBSTEPS - 1:
                finish(a, *advance(net_a, fields_a))
                load(chunk_of(jnp.minimum(a + 2, chunks - 1)), fields_a, operand_a)
            else:
                renew(net_a, fields_a, operand_a)

    leave(chunks - 3)
    leave(chunks - 2)
    for copy in sends():
        copy.wait()
    finish(chunks - 1, *advance(net_b, fields_b))
    count = 4 * width
    fields_h, operand_h, net_h = (
        ref.at[:, pl.ds(0, count)] for ref in (fields_a, operand_a, net_a)
    )
    load(jnp.concatenate([halos[place] for place in range(4)], axis=1), fields_h, operand_h)
    for _ in range(SUBSTEPS):
        rates(operand_h, net_h)
        renew(net_h, fields_h, operand_h)
    leave(chunks - 1)
    for place in range(4):
        edges[place] = fields_h[:, place * width : (place + 1) * width] * LN2
    copy = pltpu.make_async_copy(edges, halo_ref, halo_sem)
    copy.start()

    @pl.loop(0, tiles)
    def _(tile):
        flush(tile).wait()

    copy.wait()


def transport_kernel(
    state_ref,
    spread_input,
    halo_input,
    conc_ref,
    temp_ref,
    spread_ref,
    halo_ref,
    old,
    new,
    gains,
    sides,
    sheet,
    small_sem,
    in_sem,
    out_sem,
    temp_sem,
):
    species, rows, width = conc_ref.shape
    blocks = (species + 1) // BLOCK
    row = lax.broadcasted_iota(jnp.int32, (rows, width), 0)
    lane = lax.broadcasted_iota(jnp.int32, (rows, width), 1)

    def fetch(block):
        at = pl.ds(block * BLOCK, BLOCK)
        return pltpu.make_async_copy(state_ref.at[at], old.at[at], in_sem.at[block])

    def flush(block, count):
        at = pl.ds(block * BLOCK, count)
        return pltpu.make_async_copy(new.at[at], conc_ref.at[at], out_sem.at[block])

    def flush_temper():
        return pltpu.make_async_copy(new.at[species], temp_ref, temp_sem)

    smalls = [
        pltpu.make_async_copy(halo_input, halo_ref, small_sem.at[0]),
        pltpu.make_async_copy(spread_input, spread_ref, small_sem.at[1]),
    ]
    for copy in smalls:
        copy.start()

    @pl.loop(0, blocks)
    def _(block):
        fetch(block).start()

    for copy in smalls:
        copy.wait()

    def around(here, component):
        north = jnp.where(row == 0, halo_ref[UP, component], pltpu.roll(here, 1, 0))
        south = jnp.where(
            row == rows - 1, halo_ref[DOWN, component], pltpu.roll(here, rows - 1, 0)
        )
        side = pltpu.roll(sides[...], width - 1 - 2 * component, 1)
        west = jnp.where(lane == 0, side, pltpu.roll(here, 1, 1))
        east = jnp.where(lane == width - 1, side, pltpu.roll(here, width - 1, 1))
        return north, south, west, east

    sheet[...] = jnp.zeros_like(sheet)
    sheet[pl.ds(0, FIELD_ROWS, stride=2)] = halo_ref[RIGHT]
    sheet[pl.ds(1, FIELD_ROWS, stride=2)] = halo_ref[LEFT]
    sides[...] = sheet[...].T
    here = spread_ref[...]
    rest = jnp.ones_like(here)
    for index, near in enumerate(around(here, FIELD_ROWS - 2)):
        gain = (0.5 * DIFFUSION_NUMBER) * (here + near)
        gains[index] = gain
        rest = rest - gain
    gains[4] = rest

    @pl.loop(0, blocks)
    def _(block):
        fetch(block).wait()
        for index in range(BLOCK):
            component = block * BLOCK + index
            here = old[component]
            total = gains[4] * here
            for which, near in enumerate(around(here, component)):
                total = total + gains[which] * near
            new[component] = total

        @pl.when(block < blocks - 1)
        def _():
            flush(block, BLOCK).start()

    flush(blocks - 1, BLOCK - 1).start()
    flush_temper().start()

    @pl.loop(0, blocks - 1)
    def _(block):
        flush(block, BLOCK).wait()

    flush(blocks - 1, BLOCK - 1).wait()
    flush_temper().wait()


def per_device(
    molar_density_logs,
    scaled_thermal_state,
    spreading_rate,
    tile_burning_load,
    input_multipliers,
    output_multipliers,
    arrhenius_prefactor_logs,
    arrhenius_barrier,
    balance_ratio_logs,
    enthalpy_yield,
):
    rows, species, width = molar_density_logs.shape
    laws = input_multipliers.shape[0]
    padded = -(-laws // 8) * 8
    wide = -(-laws // 128) * 128
    tiles = rows // TILE
    cells = CHUNK * width
    anywhere = pl.BlockSpec(memory_space=pl.ANY)
    state, halo = pl.pallas_call(
        chemistry_kernel,
        out_shape=(
            jax.ShapeDtypeStruct((FIELD_ROWS, rows, width), F32),
            jax.ShapeDtypeStruct((4, FIELD_ROWS, width), F32),
        ),
        in_specs=[anywhere] * 10,
        out_specs=(anywhere,) * 2,
        scratch_shapes=[
            pltpu.VMEM((tiles + CHUNK // TILE, FIELD_ROWS, TILE, width), F32),
            pltpu.VMEM((1, rows), jnp.int32),
            pltpu.VMEM((species, laws), jnp.int32),
            pltpu.VMEM((species, laws), jnp.int32),
            pltpu.VMEM((laws,), F32),
            pltpu.VMEM((laws,), F32),
            pltpu.VMEM((laws,), F32),
            pltpu.VMEM((laws,), F32),
            pltpu.VMEM((4, FIELD_ROWS, width), F32),
            pltpu.VMEM((4, FIELD_ROWS, width), F32),
            pltpu.VMEM((2, FIELD_ROWS, width), F32),
            pltpu.VMEM((2 * padded, 2 * SLOTS), BF16),
            pltpu.VMEM((SLOTS, 2 * padded), BF16),
            pltpu.VMEM((8, wide), F32),
            pltpu.VMEM((2 * SLOTS, wide), F32),
            pltpu.VMEM((FIELD_ROWS, cells), F32),
            pltpu.VMEM((FIELD_ROWS, cells), F32),
            pltpu.VMEM((2 * SLOTS, cells), BF16),
            pltpu.VMEM((2 * SLOTS, cells), BF16),
            pltpu.VMEM((2 * padded, cells), BF16),
            pltpu.VMEM((2 * padded, cells), BF16),
            pltpu.SemaphoreType.DMA((7,)),
            pltpu.SemaphoreType.DMA((2,)),
            pltpu.SemaphoreType.DMA((tiles,)),
            pltpu.SemaphoreType.DMA((tiles,)),
            pltpu.SemaphoreType.DMA(()),
            pltpu.SemaphoreType.DMA((4,)),
            pltpu.SemaphoreType.DMA((4,)),
        ],
        compiler_params=pltpu.CompilerParams(
            collective_id=0, has_side_effects=True, vmem_limit_bytes=60 * 2**20
        ),
        name="chemistry",
    )(
        jnp.transpose(molar_density_logs, (1, 0, 2)),
        scaled_thermal_state,
        spreading_rate,
        tile_burning_load.reshape(1, rows),
        input_multipliers.T,
        output_multipliers.T,
        arrhenius_prefactor_logs,
        arrhenius_barrier,
        balance_ratio_logs,
        enthalpy_yield,
    )

    blocks = (species + 1) // BLOCK
    conc, temp = pl.pallas_call(
        transport_kernel,
        out_shape=(
            jax.ShapeDtypeStruct((species, rows, width), F32),
            jax.ShapeDtypeStruct((rows, width), F32),
        ),
        in_specs=[anywhere] * 3,
        out_specs=(anywhere, anywhere),
        scratch_shapes=[
            pltpu.VMEM((rows, width), F32),
            pltpu.VMEM((4, FIELD_ROWS, width), F32),
            pltpu.VMEM((species + 1, rows, width), F32),
            pltpu.VMEM((species + 1, rows, width), F32),
            pltpu.VMEM((5, rows, width), F32),
            pltpu.VMEM((rows, width), F32),
            pltpu.VMEM((width, rows), F32),
            pltpu.SemaphoreType.DMA((2,)),
            pltpu.SemaphoreType.DMA((blocks,)),
            pltpu.SemaphoreType.DMA((blocks,)),
            pltpu.SemaphoreType.DMA(()),
        ],
        compiler_params=pltpu.CompilerParams(vmem_limit_bytes=60 * 2**20),
        name="transport",
    )(state, spreading_rate, halo)
    return jnp.transpose(conc, (1, 0, 2)), temp


def solution(mesh):
    placed = (
        P("gx", None, "gy"),
        P("gx", "gy"),
        P("gx", "gy"),
        P("gx", "gy"),
        P(),
        P(),
        P(),
        P(),
        P(),
        P(),
    )
    return jax.shard_map(
        per_device,
        mesh=mesh,
        in_specs=placed,
        out_specs=(P("gx", None, "gy"), P("gx", "gy")),
        check_vma=False,
    )
```
